1024 devices in a mesh: depth: 4 (over y_hi, core), hx: 32 (over z), hy: 8 (over y_lo, x).
Axes of the slice: x: 4, y: 4 (y_hi: 2, y_lo: 2; y = y_hi * 2 + y_lo), z: 32, core: 2. Of those that a mesh axis runs over, the one named last changes fastest.
Arguments:
- fine_velocity: float32 [3, 16, 192, 3072], P(None, 'depth', 'hx', 'hy'), may hold values from -6 to 6
- fine_stress: float32 [6, 16, 192, 3072], P(None, 'depth', 'hx', 'hy'), may hold values from -3 to 3
- coarse_velocity: float32 [3, 8, 64, 1024], P(None, 'depth', 'hx', 'hy'), may hold values from -6 to 6
- coarse_stress: float32 [6, 8, 64, 1024], P(None, 'depth', 'hx', 'hy'), may hold values from -3 to 3
- iwan_states: float32 [10, 6, 16, 192, 3072], P(None, None, 'depth', 'hx', 'hy'), may hold values from -0.3 to 0.3
- fine_zones: int32 [16, 192, 3072], P('depth', 'hx', 'hy'), may hold values from 0 to 15
- coarse_zones: int32 [8, 64, 1024], P('depth', 'hx', 'hy'), may hold values from 0 to 15
- plastic: int32 [16, 192, 3072], P('depth', 'hx', 'hy'), may hold values from 0 to 1, as said below
- zone_buoyancy: float32 [16], replicated, may hold values from 0.5 to 1
- zone_lambda: float32 [16], replicated, may hold values from 0.1 to 0.3
- zone_mu: float32 [16], replicated, may hold values from 0.1 to 0.3
- iwan_share: float32 [10], replicated, may hold values from 0.3 to 3
- iwan_radius: float32 [10], replicated, may hold values from 0.01 to 0.3
Outputs:
- fine_velocity_out: float32 [3, 16, 192, 3072], P(None, 'depth', 'hx', 'hy')
- fine_stress_out: float32 [6, 16, 192, 3072], P(None, 'depth', 'hx', 'hy')
- coarse_velocity_out: float32 [3, 8, 64, 1024], P(None, 'depth', 'hx', 'hy')
- coarse_stress_out: float32 [6, 8, 64, 1024], P(None, 'depth', 'hx', 'hy')
The draws below stay inside these ranges and needn't reach their ends.
Inputs may be any that keep to these rules, and one draw needn't show every extreme that they name: `plastic`: 1 marks a cell that follows the Iwan model, 0 an elastic cell.
All inputs are finite; a program needn't handle non-finite values.
Results may differ from the reference program's by a relative error of at most 0.0001.
Values sent between devices are 32-bit elements; how exact they have to be, the bound alone decides.
No kernel may reach another device: no remote copies, remote signals or barrier semaphores. Data moves between devices by JAX's collectives and lax.ppermute only.
A program may use at most 64 MiB of HBM per device.

```python
import math
import jax
import jax.numpy as jnp
from jax import lax

STEPS = 2
SURF = 10
ZONES = 16
NX = 192
NY = 3072
NZF = 16
NXC = 64
NYC = 1024
NZC = 8


def draw_plastic(key, part):
    first_key, second_key = jax.random.split(jax.random.fold_in(key, 17))
    fault = jax.random.randint(first_key, (), 0, NX)
    columns = jnp.arange(NX, dtype=jnp.int32)
    distance = jnp.abs(columns - fault)
    limits = jnp.maximum(0, 48 - 2 * distance)
    levels = jax.random.randint(second_key, (NZF, NX, NY), 0, 64)
    return (levels < limits[None, :, None]).astype(jnp.int32)


def with_ends(entries, own_key, low, high):
    shape = entries.shape
    spot = [jax.random.randint(jax.random.fold_in(own_key, axis), (), 0, shape[axis]) for axis in range(len(shape))]
    entries = entries.at[tuple(spot)].set(low)
    longest = shape.index(max(shape))
    spot[longest] = (spot[longest] + 1) % shape[longest]
    return entries.at[tuple(spot)].set(high)


def shard_levels(own_key, shape, pieces, least, high):
    gain, own = 1.0, jax.random.fold_in(own_key, 6)
    for axis_at, shards_of in pieces:
        steps = jnp.exp(jax.random.uniform(jax.random.fold_in(own, axis_at), (shards_of,), jnp.float32, least / len(pieces), high / len(pieces)))
        gain = gain * jnp.repeat(steps, shape[axis_at] // shards_of).reshape([-1 if axis == axis_at else 1 for axis in range(len(shape))])
    return gain


def noise(key, shape, scale, most, pieces=(), held_as=jnp.bfloat16):
    gain = shard_levels(key, shape, pieces, -0.22, 0.18) if pieces else 1.0
    values = jax.random.normal(key, shape, jnp.float32) * scale * gain
    return jnp.minimum(jnp.maximum(values, -most), most).astype(held_as)


def setup_inputs(seed: int = 0) -> dict:
    key_list = jax.random.split(jax.random.key(seed), 14)
    fine_velocity = noise(key_list[0], (3, NZF, NX, NY), 1.0, 6.0, ((1, 4), (2, 32), (3, 8)), jnp.float32)
    fine_stress = noise(key_list[1], (6, NZF, NX, NY), 0.5, 3.0, ((1, 4), (2, 32), (3, 8)), jnp.float32)
    coarse_velocity = noise(key_list[2], (3, NZC, NXC, NYC), 1.0, 6.0, ((1, 4), (2, 32), (3, 8)), jnp.float32)
    coarse_stress = noise(key_list[3], (6, NZC, NXC, NYC), 0.5, 3.0, ((1, 4), (2, 32), (3, 8)), jnp.float32)
    iwan_states = noise(key_list[4], (SURF, 6, NZF, NX, NY), 0.05, 0.3, ((2, 4), (3, 32), (4, 8)), jnp.float32)
    fine_zones = with_ends(jax.random.randint(key_list[5], (NZF, NX, NY), 0, ZONES), jax.random.fold_in(key_list[5], 1), 0, ZONES - 1).astype(jnp.int32)
    coarse_zones = with_ends(jax.random.randint(key_list[6], (NZC, NXC, NYC), 0, ZONES), jax.random.fold_in(key_list[6], 1), 0, ZONES - 1).astype(jnp.int32)
    plastic = draw_plastic(jax.random.fold_in(key_list[13], 71), 0)
    zone_buoyancy = jnp.clip(jax.random.uniform(key_list[8], (ZONES,), jnp.float32, 0.5, 1.0), 0.5, 1.0)
    zone_lambda = jnp.clip(jax.random.uniform(key_list[9], (ZONES,), jnp.float32, 0.1, 0.3), 0.1, 0.3)
    zone_mu = jnp.clip(jax.random.uniform(key_list[10], (ZONES,), jnp.float32, 0.1, 0.3), 0.1, 0.3)
    iwan_share = jnp.clip(jnp.exp(jax.random.uniform(key_list[11], (SURF,), jnp.float32, math.log(0.3), math.log(3.0))), 0.3, 3.0)
    iwan_radius = jnp.clip(jnp.exp(jax.random.uniform(key_list[12], (SURF,), jnp.float32, math.log(0.01), math.log(0.3))), 0.01, 0.3)
    return dict(fine_velocity=fine_velocity, fine_stress=fine_stress, coarse_velocity=coarse_velocity, coarse_stress=coarse_stress, iwan_states=iwan_states, fine_zones=fine_zones, coarse_zones=coarse_zones, plastic=plastic, zone_buoyancy=zone_buoyancy, zone_lambda=zone_lambda, zone_mu=zone_mu, iwan_share=iwan_share, iwan_radius=iwan_radius)


step_time = 0.4
near_coef = 9.0 / 8.0
far_coef = 1.0 / 24.0

def shifted(padded, along, offset):
    length = padded.shape[along] - 4
    return lax.slice_in_dim(padded, 2 + offset, 2 + offset + length, axis=along)

def derivative(padded, along, forward, spacing):
    if forward:
        value = near_coef * (shifted(padded, along, 1) - shifted(padded, along, 0)) - far_coef * (shifted(padded, along, 2) - shifted(padded, along, -1))
    else:
        value = near_coef * (shifted(padded, along, 0) - shifted(padded, along, -1)) - far_coef * (shifted(padded, along, 1) - shifted(padded, along, -2))
    return value / spacing

def inner(padded, dims):
    for other in dims:
        padded = lax.slice_in_dim(padded, 2, padded.shape[other] - 2, axis=other)
    return padded

def lookup(zone_ids, values):
    total = jnp.zeros(zone_ids.shape, jnp.float32)
    for member in range(values.shape[0]):
        total = total + jnp.where(zone_ids == member, values[member], jnp.float32(0.0))
    return total

def spread(plane):
    return jnp.repeat(jnp.repeat(plane, 3, axis=-2), 3, axis=-1)

def shrink(plane):
    shape = plane.shape
    return plane.reshape(shape[:-2] + (shape[-2] // 3, 3, shape[-1] // 3, 3)).mean(axis=(-3, -1))

def whole_getter(padded):

    def getter(component, along):
        return inner(padded[component], [other for other in (0, 1, 2) if other != along])
    return getter

def velocity_step(velocity, getter, buoyancy, spacing):
    force_x = derivative(getter(0, 1), 1, True, spacing) + derivative(getter(3, 2), 2, False, spacing) + derivative(getter(4, 0), 0, False, spacing)
    force_y = derivative(getter(3, 1), 1, False, spacing) + derivative(getter(1, 2), 2, True, spacing) + derivative(getter(5, 0), 0, False, spacing)
    force_z = derivative(getter(4, 1), 1, False, spacing) + derivative(getter(5, 2), 2, False, spacing) + derivative(getter(2, 0), 0, True, spacing)
    return velocity + step_time * buoyancy[None] * jnp.stack([force_x, force_y, force_z])

def strain_rates(padded, spacing):
    getter = whole_getter(padded)

    def rate(component, along, forward):
        return derivative(getter(component, along), along, forward, spacing)
    rate_xx = rate(0, 1, False)
    rate_yy = rate(1, 2, False)
    rate_zz = rate(2, 0, False)
    rate_xy = rate(1, 1, True) + rate(0, 2, True)
    rate_xz = rate(2, 1, True) + rate(0, 0, True)
    rate_yz = rate(2, 2, True) + rate(1, 0, True)
    return [rate_xx, rate_yy, rate_zz, rate_xy, rate_xz, rate_yz]

def elastic_stress(stress, rates, lame_first, shear_mod):
    dilation = rates[0] + rates[1] + rates[2]
    normal = [stress[member] + step_time * (lame_first * dilation + 2.0 * shear_mod * rates[member]) for member in range(3)]
    shear = [stress[member] + step_time * shear_mod * rates[member] for member in range(3, 6)]
    return jnp.stack(normal + shear)

def deviator_increment(rates, shear_mod):
    dilation = rates[0] + rates[1] + rates[2]
    normal = [2.0 * shear_mod * step_time * (rates[member] - dilation / 3.0) for member in range(3)]
    shear = [shear_mod * step_time * rates[member] for member in range(3, 6)]
    return jnp.stack(normal + shear)

def plastic_stress(stress, rates, lame_first, shear_mod, deviator):
    dilation = rates[0] + rates[1] + rates[2]
    mean_part = (stress[0] + stress[1] + stress[2]) / 3.0 + step_time * (lame_first + 2.0 * shear_mod / 3.0) * dilation
    return jnp.stack([mean_part + deviator[0], mean_part + deviator[1], mean_part + deviator[2], deviator[3], deviator[4], deviator[5]])

def iwan_return(states, increment, weights, radius):
    trial_state = states + weights[:, None, None, None, None] * increment[None]
    magnitude = jnp.sqrt(0.5 * (trial_state[:, 0] ** 2 + trial_state[:, 1] ** 2 + trial_state[:, 2] ** 2) + trial_state[:, 3] ** 2 + trial_state[:, 4] ** 2 + trial_state[:, 5] ** 2)
    limits = radius[:, None, None, None]
    scaled = trial_state * (limits / jnp.maximum(magnitude, limits))[:, None]
    return (scaled, lax.optimization_barrier(jnp.sum(scaled, axis=0)))

def attach_below(padded, rows, ghosts, flag, margin):
    depth_len = padded.shape[1]
    picks = jnp.array(rows, dtype=jnp.int32)
    for offset in range(2):
        old = padded[picks, depth_len - 2 + offset, margin:padded.shape[2] - margin, margin:padded.shape[3] - margin]
        padded = padded.at[picks, depth_len - 2 + offset, margin:padded.shape[2] - margin, margin:padded.shape[3] - margin].set(jnp.where(flag, ghosts[offset], old))
    return padded

def attach_above(padded, rows, ghosts, flag, margin):
    picks = jnp.array(rows, dtype=jnp.int32)
    for offset in range(2):
        old = padded[picks, 1 - offset, margin:padded.shape[2] - margin, margin:padded.shape[3] - margin]
        padded = padded.at[picks, 1 - offset, margin:padded.shape[2] - margin, margin:padded.shape[3] - margin].set(jnp.where(flag, ghosts[offset], old))
    return padded

def pad_all(stack):
    return jnp.pad(stack, ((0, 0), (2, 2), (2, 2), (2, 2)))

def join_grids(fine_pad, coarse_pad, fine_full, coarse_full, rows):
    picks = jnp.array(rows, dtype=jnp.int32)
    fine_rows = fine_full[picks]
    coarse_rows = coarse_full[picks]
    below = spread(coarse_rows[:, 0])
    bottom = fine_rows[:, -1]
    ghosts = [2.0 / 3.0 * bottom + 1.0 / 3.0 * below, 1.0 / 3.0 * bottom + 2.0 / 3.0 * below]
    above = shrink(jnp.stack([fine_rows[:, -1], fine_rows[:, -4]]))
    fine_pad = attach_below(fine_pad, rows, ghosts, True, 2)
    coarse_pad = attach_above(coarse_pad, rows, above, True, 2)
    return (fine_pad, coarse_pad)

def reference(fine_velocity, fine_stress, coarse_velocity, coarse_stress, iwan_states, fine_zones, coarse_zones, plastic, zone_buoyancy, zone_lambda, zone_mu, iwan_share, iwan_radius):
    coarse_velocity = jnp.flip(coarse_velocity, 1)
    coarse_stress = jnp.flip(coarse_stress, 1)
    coarse_zones = jnp.flip(coarse_zones, 0)
    fine_buoyancy = lookup(fine_zones, zone_buoyancy)
    fine_lame = lookup(fine_zones, zone_lambda)
    fine_shear = lookup(fine_zones, zone_mu)
    coarse_buoyancy = lookup(coarse_zones, zone_buoyancy)
    coarse_lame = lookup(coarse_zones, zone_lambda)
    coarse_shear = lookup(coarse_zones, zone_mu)
    weights = iwan_share / jnp.sum(iwan_share)
    active = plastic == 1
    states = iwan_states
    for step in range(STEPS):
        fine_pad, coarse_pad = join_grids(pad_all(fine_stress), pad_all(coarse_stress), fine_stress, coarse_stress, (2, 4, 5))
        fine_velocity = velocity_step(fine_velocity, whole_getter(fine_pad), fine_buoyancy, 1.0)
        coarse_velocity = velocity_step(coarse_velocity, whole_getter(coarse_pad), coarse_buoyancy, 3.0)
        fine_pad, coarse_pad = join_grids(pad_all(fine_velocity), pad_all(coarse_velocity), fine_velocity, coarse_velocity, (0, 1, 2))
        fine_rates = strain_rates(fine_pad, 1.0)
        elastic = elastic_stress(fine_stress, fine_rates, fine_lame, fine_shear)
        increment = deviator_increment(fine_rates, fine_shear)

        def plane_update(member, carry):
            states_now, deviator_now = carry
            part_states = lax.dynamic_slice_in_dim(states_now, member, 1, 2)
            part_increment = lax.dynamic_slice_in_dim(increment, member, 1, 1)
            part_active = lax.dynamic_slice_in_dim(active, member, 1, 0)
            scaled, deviator = iwan_return(part_states, part_increment, weights, iwan_radius)
            kept = jnp.where(part_active[None, None], scaled, part_states)
            states_now = lax.dynamic_update_slice_in_dim(states_now, kept, member, 2)
            deviator_now = lax.dynamic_update_slice_in_dim(deviator_now, deviator, member, 1)
            return (states_now, deviator_now)
        states, deviator_all = lax.fori_loop(0, fine_stress.shape[1], plane_update, (states, jnp.zeros_like(increment)))
        yielded = plastic_stress(fine_stress, fine_rates, fine_lame, fine_shear, deviator_all)
        fine_stress = jnp.where(active[None], yielded, elastic)
        coarse_rates = strain_rates(coarse_pad, 3.0)
        coarse_stress = elastic_stress(coarse_stress, coarse_rates, coarse_lame, coarse_shear)
    return (fine_velocity, fine_stress, jnp.flip(coarse_velocity, 1), jnp.flip(coarse_stress, 1))
```

```python
import jax
import jax.numpy as jnp
from jax import lax
from jax.sharding import PartitionSpec as P

STEPS = 2


step_time = 0.4
near_coef = 9.0 / 8.0
far_coef = 1.0 / 24.0


def padded_2(x, sides, width):
    edges = {}
    for axis, dim in sides:
        count, length = (lax.axis_size(axis), x.shape[dim])
        up = [(i, (i + 1) % count) for i in range(count - 1)]
        last = lax.slice_in_dim(x, length - width, length, axis=dim)
        first = lax.slice_in_dim(x, 0, width, axis=dim)
        edges[dim] = (
            lax.ppermute(last, axis, up),
            lax.ppermute(first, axis, [(b, a) for a, b in up]),
        )
    done = []
    for _, dim in sides:
        low, high = edges[dim]
        around = [(width, width) if d in done else (0, 0) for d in range(x.ndim)]
        x = jnp.concatenate([jnp.pad(low, around), x, jnp.pad(high, around)], axis=dim)
        done.append(dim)
    return x


def padded_3(x, sides, width):
    for axis, dim in sides:
        count, length = (lax.axis_size(axis), x.shape[dim])
        up = [(i, (i + 1) % count) for i in range(count - 1)]
        down = [(j, i) for i, j in up]
        last = lax.slice_in_dim(x, length - width, length, axis=dim)
        first = lax.slice_in_dim(x, 0, width, axis=dim)
        before = lax.ppermute(last, axis, up)
        after = lax.ppermute(first, axis, down)
        x = jnp.concatenate([before, x, after], axis=dim)
    return x


def shifted(padded, along, offset):
    length = padded.shape[along] - 4
    return lax.slice_in_dim(padded, 2 + offset, 2 + offset + length, axis=along)


def derivative(padded, along, forward, spacing):
    if forward:
        value = near_coef * (shifted(padded, along, 1) - shifted(padded, along, 0)) - far_coef * (
            shifted(padded, along, 2) - shifted(padded, along, -1)
        )
    else:
        value = near_coef * (shifted(padded, along, 0) - shifted(padded, along, -1)) - far_coef * (
            shifted(padded, along, 1) - shifted(padded, along, -2)
        )
    return value / spacing


def inner(padded, dims):
    for other in dims:
        padded = lax.slice_in_dim(padded, 2, padded.shape[other] - 2, axis=other)
    return padded


def lookup(zone_ids, values):
    total = jnp.zeros(zone_ids.shape, jnp.float32)
    for member in range(values.shape[0]):
        total = total + jnp.where(zone_ids == member, values[member], jnp.float32(0.0))
    return total


def spread(plane):
    return jnp.repeat(jnp.repeat(plane, 3, axis=-2), 3, axis=-1)


def shrink(plane):
    shape = plane.shape
    return plane.reshape(shape[:-2] + (shape[-2] // 3, 3, shape[-1] // 3, 3)).mean(axis=(-3, -1))


def whole_getter(padded):

    def getter(component, along):
        return inner(padded[component], [other for other in (0, 1, 2) if other != along])

    return getter


def velocity_step(velocity, getter, buoyancy, spacing):
    force_x = (
        derivative(getter(0, 1), 1, True, spacing)
        + derivative(getter(3, 2), 2, False, spacing)
        + derivative(getter(4, 0), 0, False, spacing)
    )
    force_y = (
        derivative(getter(3, 1), 1, False, spacing)
        + derivative(getter(1, 2), 2, True, spacing)
        + derivative(getter(5, 0), 0, False, spacing)
    )
    force_z = (
        derivative(getter(4, 1), 1, False, spacing)
        + derivative(getter(5, 2), 2, False, spacing)
        + derivative(getter(2, 0), 0, True, spacing)
    )
    return velocity + step_time * buoyancy[None] * jnp.stack([force_x, force_y, force_z])


def strain_rates(padded, spacing):
    getter = whole_getter(padded)

    def rate(component, along, forward):
        return derivative(getter(component, along), along, forward, spacing)

    rate_xx = rate(0, 1, False)
    rate_yy = rate(1, 2, False)
    rate_zz = rate(2, 0, False)
    rate_xy = rate(1, 1, True) + rate(0, 2, True)
    rate_xz = rate(2, 1, True) + rate(0, 0, True)
    rate_yz = rate(2, 2, True) + rate(1, 0, True)
    return [rate_xx, rate_yy, rate_zz, rate_xy, rate_xz, rate_yz]


def elastic_stress(stress, rates, lame_first, shear_mod):
    dilation = rates[0] + rates[1] + rates[2]
    normal = [
        stress[member] + step_time * (lame_first * dilation + 2.0 * shear_mod * rates[member])
        for member in range(3)
    ]
    shear = [stress[member] + step_time * shear_mod * rates[member] for member in range(3, 6)]
    return jnp.stack(normal + shear)


def deviator_increment(rates, shear_mod):
    dilation = rates[0] + rates[1] + rates[2]
    normal = [2.0 * shear_mod * step_time * (rates[member] - dilation / 3.0) for member in range(3)]
    shear = [shear_mod * step_time * rates[member] for member in range(3, 6)]
    return jnp.stack(normal + shear)


def plastic_stress(stress, rates, lame_first, shear_mod, deviator):
    dilation = rates[0] + rates[1] + rates[2]
    mean_part = (stress[0] + stress[1] + stress[2]) / 3.0 + step_time * (
        lame_first + 2.0 * shear_mod / 3.0
    ) * dilation
    return jnp.stack(
        [
            mean_part + deviator[0],
            mean_part + deviator[1],
            mean_part + deviator[2],
            deviator[3],
            deviator[4],
            deviator[5],
        ]
    )


def iwan_return(states, increment, weights, radius):
    trial_state = states + weights[:, None, None, None, None] * increment[None]
    magnitude = jnp.sqrt(
        0.5 * (trial_state[:, 0] ** 2 + trial_state[:, 1] ** 2 + trial_state[:, 2] ** 2)
        + trial_state[:, 3] ** 2
        + trial_state[:, 4] ** 2
        + trial_state[:, 5] ** 2
    )
    limits = radius[:, None, None, None]
    scaled = trial_state * (limits / jnp.maximum(magnitude, limits))[:, None]
    return (scaled, jnp.sum(scaled, axis=0))


def attach(padded, rows, ghosts, flag, margin, planes):
    mid = (slice(margin, padded.shape[2] - margin), slice(margin, padded.shape[3] - margin))
    for offset in range(2):
        for place, row in enumerate(rows):
            spot = (row, planes[offset]) + mid
            padded = padded.at[spot].set(jnp.where(flag, ghosts[offset][place], padded[spot]))
    return padded


def attach_below(padded, rows, ghosts, flag, margin):
    depth_len = padded.shape[1]
    return attach(padded, rows, ghosts, flag, margin, (depth_len - 2, depth_len - 1))


def attach_above(padded, rows, ghosts, flag, margin):
    return attach(padded, rows, ghosts, flag, margin, (1, 0))


def coarse_halo(stack):
    stored = jnp.flip(stack, 1)
    padded = padded_2(stored, (("depth", 1), ("hx", 2), ("hy", 3)), 2)
    return jnp.flip(padded, 1)


def couple(fine_rows, coarse_rows):
    prolonged = spread(coarse_rows[:, 0])
    above = shrink(jnp.stack([fine_rows[:, -1], fine_rows[:, -4]]))
    bottom = fine_rows[:, -1]
    ghosts = [
        2.0 / 3.0 * bottom + 1.0 / 3.0 * prolonged,
        1.0 / 3.0 * bottom + 2.0 / 3.0 * prolonged,
    ]
    return (ghosts, above)


def per_device(
    fine_velocity,
    fine_stress,
    coarse_velocity,
    coarse_stress,
    iwan_states,
    fine_zones,
    coarse_zones,
    plastic,
    zone_buoyancy,
    zone_lambda,
    zone_mu,
    iwan_share,
    iwan_radius,
):
    coarse_velocity = jnp.flip(coarse_velocity, 1)
    coarse_stress = jnp.flip(coarse_stress, 1)
    coarse_zones = jnp.flip(coarse_zones, 0)
    fine_buoyancy = lookup(fine_zones, zone_buoyancy)
    fine_lame = lookup(fine_zones, zone_lambda)
    fine_shear = lookup(fine_zones, zone_mu)
    coarse_buoyancy = lookup(coarse_zones, zone_buoyancy)
    coarse_lame = lookup(coarse_zones, zone_lambda)
    coarse_shear = lookup(coarse_zones, zone_mu)
    weights = iwan_share / jnp.sum(iwan_share)
    active = plastic == 1
    states = iwan_states
    groups = lax.axis_size("depth")
    place = lax.axis_index("depth")
    is_bottom = place == groups - 1
    for step in range(STEPS):
        coarse_pad = coarse_halo(coarse_stress)
        ghosts, above = couple(
            jnp.stack([fine_stress[2], fine_stress[4], fine_stress[5]]),
            jnp.stack([coarse_stress[2], coarse_stress[4], coarse_stress[5]]),
        )
        coarse_pad = attach_above(coarse_pad, (2, 4, 5), above, is_bottom, 2)
        padded_x = padded_3(
            jnp.stack([fine_stress[0], fine_stress[3], fine_stress[4]]), (("hx", 2),), 2
        )
        padded_y = padded_3(
            jnp.stack([fine_stress[1], fine_stress[3], fine_stress[5]]), (("hy", 3),), 2
        )
        padded_z = padded_3(
            jnp.stack([fine_stress[2], fine_stress[4], fine_stress[5]]), (("depth", 1),), 2
        )
        padded_z = attach_below(padded_z, (0, 1, 2), ghosts, is_bottom, 0)
        by_direction = {
            1: (padded_x, {0: 0, 3: 1, 4: 2}),
            2: (padded_y, {1: 0, 3: 1, 5: 2}),
            0: (padded_z, {2: 0, 4: 1, 5: 2}),
        }

        def fine_getter(component, along):
            padded, places = by_direction[along]
            return padded[places[component]]

        fine_velocity = velocity_step(fine_velocity, fine_getter, fine_buoyancy, 1.0)
        coarse_velocity = velocity_step(
            coarse_velocity, whole_getter(coarse_pad), coarse_buoyancy, 3.0
        )
        velocity_pad = padded_2(fine_velocity, (("depth", 1), ("hx", 2), ("hy", 3)), 2)
        coarse_pad = coarse_halo(coarse_velocity)
        ghosts, above = couple(fine_velocity, coarse_velocity)
        velocity_pad = attach_below(velocity_pad, (0, 1, 2), ghosts, is_bottom, 2)
        coarse_pad = attach_above(coarse_pad, (0, 1, 2), above, is_bottom, 2)
        fine_rates = strain_rates(velocity_pad, 1.0)
        elastic = elastic_stress(fine_stress, fine_rates, fine_lame, fine_shear)
        increment = deviator_increment(fine_rates, fine_shear)
        scaled, deviator_all = iwan_return(states, increment, weights, iwan_radius)
        states = jnp.where(active[None, None], scaled, states)
        yielded = plastic_stress(fine_stress, fine_rates, fine_lame, fine_shear, deviator_all)
        fine_stress = jnp.where(active[None], yielded, elastic)
        coarse_rates = strain_rates(coarse_pad, 3.0)
        coarse_stress = elastic_stress(coarse_stress, coarse_rates, coarse_lame, coarse_shear)
    return (fine_velocity, fine_stress, jnp.flip(coarse_velocity, 1), jnp.flip(coarse_stress, 1))


def solution(mesh):
    return jax.shard_map(
        per_device,
        mesh=mesh,
        in_specs=(
            P(None, "depth", "hx", "hy"),
            P(None, "depth", "hx", "hy"),
            P(None, "depth", "hx", "hy"),
            P(None, "depth", "hx", "hy"),
            P(None, None, "depth", "hx", "hy"),
            P("depth", "hx", "hy"),
            P("depth", "hx", "hy"),
            P("depth", "hx", "hy"),
            P(),
            P(),
            P(),
            P(),
            P(),
        ),
        out_specs=(
            P(None, "depth", "hx", "hy"),
            P(None, "depth", "hx", "hy"),
            P(None, "depth", "hx", "hy"),
            P(None, "depth", "hx", "hy"),
        ),
        check_vma=False,
    )
```

```python
import functools

import jax
import jax.numpy as jnp
from jax import lax
from jax.experimental import pallas as pl
from jax.experimental.pallas import tpu as pltpu
from jax.sharding import PartitionSpec as P

DT = 0.4
NEAR = 9.0 / 8.0
FAR = 1.0 / 24.0
F32 = jnp.float32
ROWS, LANES = 6, 384
TILE = 128
STRESS = {"x": (0, 3, 4), "y": (1, 3, 5), "z": (2, 4, 5)}
SPEED = {"x": (0, 1, 2), "y": (0, 1, 2), "z": (0, 1, 2)}
MESSAGES = {"x": (4, 8, LANES), "y": (4, 8, TILE), "z": (6, 8, LANES)}


def roll(x, shift, axis):
    shift %= x.shape[axis]
    return x if shift == 0 else pltpu.roll(x, shift, axis)


def iota(shape, axis):
    return lax.broadcasted_iota(jnp.int32, shape, axis)


def stencil(get, forward, scale):
    near, far = NEAR * scale, FAR * scale
    if forward:
        return near * (get(1) - get(0)) - far * (get(2) - get(-1))
    return near * (get(0) - get(-1)) - far * (get(1) - get(-2))


def lookup(zones, table):
    total = jnp.zeros(zones.shape, F32)
    for member in range(table.shape[0]):
        total = jnp.where(zones == member, table[member], total)
    return total


class Fields:
    def __init__(self, fine, coarse, fine_room, coarse_room, sets, halos):
        self.fine_room, self.coarse_room, self.sets, self.halos = fine_room, coarse_room, sets, halos
        for c in range(fine.shape[0]):
            for z in range(4):
                fine_room[c, z, 0:ROWS] = fine[c, z]
                fine_room[c, z, ROWS:8] = jnp.zeros((2, LANES), F32)
            for z in range(2):
                coarse_room[c, z] = jnp.zeros((8, TILE), F32)
                coarse_room[c, z, 0:2] = coarse[c, 1 - z]

    def couple(self):
        bottom = (lax.axis_index("depth") == lax.axis_size("depth") - 1).astype(F32)
        comps = self.sets["z"]
        narrow, wide = iota((TILE, LANES), 0) * 3, iota((TILE, LANES), 1)
        repeat = jnp.where((wide >= narrow) & (wide < narrow + 3), 1.0, 0.0).astype(F32)
        narrow, wide = iota((LANES, TILE), 1) * 3, iota((LANES, TILE), 0)
        gather = jnp.where((wide >= narrow) & (wide < narrow + 3), bottom / 9.0, 0.0).astype(F32)
        dot = functools.partial(
            jnp.dot, precision=lax.Precision.HIGHEST, preferred_element_type=F32
        )
        row = iota((8, LANES), 0)
        self.below, self.above = {}, {}
        spread = dot(jnp.concatenate([self.coarse_room[c, 0] for c in comps], 0), repeat)
        means = dot(
            jnp.concatenate([self.fine_room[c, z] for c in comps for z in (3, 0)], 0), gather
        )
        for place, c in enumerate(comps):
            wide = spread[8 * place : 8 * place + 8]
            wide = jnp.where(row < 3, wide[0:1], wide[1:2])
            last = self.fine_room[c, 3]
            self.below[c, 4] = bottom * (2.0 / 3.0 * last + 1.0 / 3.0 * wide)
            self.below[c, 5] = bottom * (1.0 / 3.0 * last + 2.0 / 3.0 * wide)
            for step in range(2):
                at = 8 * (2 * place + step)
                part = means[at : at + 8]
                part = part + roll(part, -1, 0) + roll(part, -2, 0)
                self.above[c, -1 - step] = jnp.where(row[:, :TILE] == 0, part, roll(part, -2, 0))

    def fine_x(self, c, z):
        place = self.sets["x"].index(c)
        row = iota((8, LANES), 0)
        own = self.fine_room[c, z]
        before = jnp.where(row < ROWS, own, roll(self.halos["x"][0][place], 6 - 2 * z, 0))
        after = jnp.where(row < ROWS, own, roll(self.halos["x"][1][place], 6 - 2 * z, 0))
        return lambda off: own if off == 0 else roll(before if off < 0 else after, -off, 0)

    def fine_y(self, c, z):
        place = self.sets["y"].index(c)
        lane = iota((8, TILE), 1)
        before = roll(self.halos["y"][0][z], 2 * place, 1)
        after = roll(self.halos["y"][1][z], -2 * place, 1)
        whole = jnp.concatenate([self.fine_room[c, z], jnp.where(lane < 64, after, before)], 1)
        return lambda off: roll(whole, -off, 1)[:, :LANES]

    def fine_z(self, c, z):
        place = self.sets["z"].index(c)

        def get(off):
            at = z + off
            if at < 0:
                return self.halos["z"][0][2 * place + at + 2]
            if at < 4:
                return self.fine_room[c, at]
            return self.halos["z"][1][2 * place + at - 4] + self.below[c, at]

        return get

    def coarse_x(self, c, z):
        place = self.sets["x"].index(c)
        lanes = slice(place * TILE, place * TILE + TILE)
        row = iota((8, TILE), 0)
        before, after = self.halos["x"][0][3, :, lanes], self.halos["x"][1][3, :, lanes]
        own = self.coarse_room[c, z]
        whole = jnp.where(row < 4, roll(after, 2 - 2 * z, 0), roll(before, 6 - 2 * z, 0))
        whole = jnp.where(row < 2, own, whole)
        return lambda off: roll(whole, -off, 0)

    def coarse_y(self, c, z):
        place = self.sets["y"].index(c)
        lane = iota((8, TILE), 1)
        before = roll(roll(self.halos["y"][0][z], 2 * place, 1), 2, 0)
        after = roll(roll(self.halos["y"][1][z], -2 * place, 1), 2, 0)
        whole = jnp.concatenate([self.coarse_room[c, z], jnp.where(lane < 64, after, before)], 1)
        return lambda off: roll(whole, -off, 1)[:, :TILE]

    def coarse_z(self, c, z):
        place = self.sets["z"].index(c)
        lanes = slice(place * TILE, place * TILE + TILE)

        def get(off):
            at = z + off
            if at < 0:
                return roll(self.halos["z"][1][at + 2, :, lanes], 2, 0) + self.above[c, at]
            if at < 2:
                return self.coarse_room[c, at]
            return roll(self.halos["z"][0][at - 2, :, lanes], 2, 0)

        return get


def pack(fine, coarse, sets, out):
    for place, c in enumerate(sets["x"]):
        for z in range(4):
            slab = fine(c, z)
            out["x"][0][place, 2 * z : 2 * z + 2] = slab[0:2]
            out["x"][1][place, 2 * z : 2 * z + 2] = slab[4:6]
    for way in range(2):
        out["x"][way][3, 4:8] = jnp.zeros((4, LANES), F32)
        for place, c in enumerate(sets["x"]):
            for z in range(2):
                out["x"][way][3, 2 * z : 2 * z + 2, place * TILE : place * TILE + TILE] = coarse(c, z)
        for place, c in enumerate(sets["z"]):
            for layer in range(2):
                at = 2 * place + layer
                out["z"][way][at, 0:ROWS] = fine(c, layer + 2 * way)
                if place:
                    out["z"][way][at, ROWS:8] = jnp.zeros((2, LANES), F32)
                out["z"][way][layer, ROWS:8, place * TILE : place * TILE + TILE] = coarse(c, layer)
        for z in range(4):
            lane = iota((ROWS, TILE), 1)
            edge = slice(0, TILE) if way == 0 else slice(LANES - TILE, LANES)
            first, second, third = [fine(c, z)[:, edge] for c in sets["y"]]
            out["y"][way][z, 0:ROWS] = columns(first, second, third, lane, way)
            if z < 2:
                lane = iota((2, TILE), 1)
                first, second, third = [coarse(c, z) for c in sets["y"]]
                out["y"][way][z, ROWS:8] = columns(first, second, third, lane, way)
            else:
                out["y"][way][z, ROWS:8] = jnp.zeros((2, TILE), F32)


def columns(first, second, third, lane, way):
    if way == 0:
        return jnp.where(lane < 2, first, jnp.where(lane < 4, roll8(second, 2), roll8(third, 4)))
    return jnp.where(lane >= 126, first, jnp.where(lane >= 124, roll8(second, -2), roll8(third, -4)))


def roll8(x, shift):
    rows = x.shape[0]
    full = jnp.concatenate([x] * (8 // rows) + ([x[: 8 % rows]] if 8 % rows else []), 0)
    return roll(full, shift, 1)[:rows]


def both(refs):
    return {"x": refs[0:2], "y": refs[2:4], "z": refs[4:6]}


def first_kernel(fs, cs, *out):
    pack(lambda c, z: fs[c, z], lambda c, z: cs[c, 1 - z], STRESS, both(out))


def velocity_kernel(fv, cv, fs, cs, fzone, czone, table, *rest):
    halos, (nfv, ncv, *out), (fine_room, coarse_room) = rest[:6], rest[6:14], rest[14:]
    f = Fields(fs, cs, fine_room, coarse_room, STRESS, both(halos))
    f.couple()

    def forces(x, y, z, scale):
        def go(of, c, forward):
            return stencil(of(c), forward, scale)

        return (
            go(x, 0, True) + go(y, 3, False) + go(z, 4, False),
            go(x, 3, False) + go(y, 1, True) + go(z, 5, False),
            go(x, 4, False) + go(y, 5, False) + go(z, 2, True),
        )

    for at in range(4):
        gain = DT * lookup(fzone[at], table)
        found = forces(*[lambda c, of=of: of(c, at) for of in (f.fine_x, f.fine_y, f.fine_z)], 1.0)
        for c in range(3):
            nfv[c, at] = fv[c, at] + gain * found[c][0:ROWS]
    for at in range(2):
        gain = DT * lookup(czone[1 - at], table)
        found = forces(
            *[lambda c, of=of: of(c, at) for of in (f.coarse_x, f.coarse_y, f.coarse_z)], 1.0 / 3.0
        )
        for c in range(3):
            ncv[c, 1 - at] = cv[c, 1 - at] + gain * found[c][0:2]
    pack(lambda c, z: nfv[c, z], lambda c, z: ncv[c, 1 - z], SPEED, both(out))


def stress_kernel(
    last, fv, cv, fs, cs, fzone, czone, plastic, states, lame, shear, share, radius, *rest
):
    halos, rest = rest[:6], rest[6:]
    nfs, ncs = rest[:2]
    out, new_states = (None, None) if last else (rest[3:9], rest[2])
    fine_room, coarse_room = rest[-2:]
    f = Fields(fv, cv, fine_room, coarse_room, SPEED, both(halos))
    f.couple()
    whole = share[0]
    for k in range(1, share.shape[0]):
        whole = whole + share[k]
    per_share = 1.0 / jnp.full((8, TILE), whole, F32)
    per_share = jnp.concatenate([per_share] * 3, 1)[0:ROWS]

    def rates(x, y, z, scale):
        def go(of, c, forward):
            return stencil(of(c), forward, scale)

        return (
            go(x, 0, False),
            go(y, 1, False),
            go(z, 2, False),
            go(x, 1, True) + go(y, 0, True),
            go(x, 2, True) + go(z, 0, True),
            go(y, 2, True) + go(z, 1, True),
        )

    for at in range(4):
        e = rates(*[lambda c, of=of: of(c, at) for of in (f.fine_x, f.fine_y, f.fine_z)], 1.0)
        e = [part[0:ROWS] for part in e]
        zone = fzone[at]
        first, mu = lookup(zone, lame), lookup(zone, shear)
        twice = (2.0 * DT) * mu
        once = DT * mu
        dilation = e[0] + e[1] + e[2]
        third = dilation * (1.0 / 3.0)
        old = [fs[c, at] for c in range(6)]
        pressure = DT * first * dilation
        rise = [twice * e[c] for c in range(3)] + [once * e[c] for c in range(3, 6)]
        elastic = [old[c] + pressure + rise[c] for c in range(3)] + [old[c] + rise[c] for c in range(3, 6)]
        step = [twice * (e[c] - third) for c in range(3)] + rise[3:]
        step = [per_share * part for part in step]
        active = plastic[at] == 1
        sums = [jnp.zeros((ROWS, LANES), F32)] * 6
        for k in range(share.shape[0]):
            weight, limit = share[k], radius[k]
            before = [states[k, c, at] for c in range(6)]
            t = [before[c] + weight * step[c] for c in range(6)]
            size = 0.5 * (t[0] * t[0] + t[1] * t[1] + t[2] * t[2]) + (
                t[3] * t[3] + t[4] * t[4] + t[5] * t[5]
            )
            back = limit * lax.rsqrt(jnp.maximum(size, limit * limit))
            t = [part * back for part in t]
            sums = [a + b for a, b in zip(sums, t)]
            if not last:
                for c in range(6):
                    new_states[k, c, at] = jnp.where(active, t[c], before[c])
        mean = (old[0] + old[1] + old[2]) * (1.0 / 3.0) + (DT * first + twice * (1.0 / 3.0)) * dilation
        for c in range(6):
            nfs[c, at] = jnp.where(active, mean + sums[c] if c < 3 else sums[c], elastic[c])
    for at in range(2):
        e = rates(
            *[lambda c, of=of: of(c, at) for of in (f.coarse_x, f.coarse_y, f.coarse_z)], 1.0 / 3.0
        )
        e = [part[0:2] for part in e]
        zone = czone[1 - at]
        first, mu = lookup(zone, lame), lookup(zone, shear)
        pressure = DT * first * (e[0] + e[1] + e[2])
        for c in range(6):
            rise = (2.0 * DT if c < 3 else DT) * mu * e[c]
            ncs[c, 1 - at] = cs[c, 1 - at] + (pressure + rise if c < 3 else rise)
    if not last:
        pack(lambda c, z: nfs[c, z], lambda c, z: ncs[c, 1 - z], STRESS, both(out))


VMEM = pl.BlockSpec(memory_space=pltpu.VMEM)
SMEM = pl.BlockSpec(memory_space=pltpu.SMEM)
SENT = [jax.ShapeDtypeStruct(MESSAGES[d], F32) for d in "xyz" for _ in range(2)]


def call(body, operands, scalars, halos, outs, rooms, flops):
    shapes = [jax.ShapeDtypeStruct(s, F32) if isinstance(s, tuple) else s for s in outs]
    return pl.pallas_call(
        body,
        out_shape=shapes,
        in_specs=[VMEM] * len(operands) + [SMEM] * len(scalars) + [VMEM] * len(halos),
        out_specs=[VMEM] * len(shapes),
        scratch_shapes=[
            s for n in rooms for s in (pltpu.VMEM((n, 4, 8, LANES), F32), pltpu.VMEM((n, 2, 8, TILE), F32))
        ],
        compiler_params=pltpu.CompilerParams(vmem_limit_bytes=40 * 2**20),
        cost_estimate=pl.CostEstimate(flops=flops, bytes_accessed=flops, transcendentals=0),
    )(*operands, *scalars, *halos)


def exchange(sent):
    found = []
    for number, axis in enumerate(("hx", "hy", "depth")):
        back, on = sent[2 * number : 2 * number + 2]
        up = [(i, i + 1) for i in range(lax.axis_size(axis) - 1)]
        found.append(lax.ppermute(on, axis, up))
        found.append(lax.ppermute(back, axis, [(b, a) for a, b in up]))
    return found


def per_device(fv, fs, cv, cs, states, fzone, czone, plastic, buoyancy, lame, shear, share, radius):
    sent = call(first_kernel, [fs, cs], [], [], SENT, [], 10**5)
    for step in range(2):
        last = step == 1
        fv, cv, *sent = call(
            velocity_kernel,
            [fv, cv, fs, cs, fzone, czone],
            [buoyancy],
            exchange(sent),
            [fv.shape, cv.shape] + SENT,
            [6],
            10**6,
        )
        found = call(
            functools.partial(stress_kernel, last),
            [fv, cv, fs, cs, fzone, czone, plastic, states],
            [lame, shear, share, radius],
            exchange(sent),
            [fs.shape, cs.shape] + ([] if last else [states.shape] + SENT),
            [3],
            10**7,
        )
        if last:
            fs, cs = found
        else:
            fs, cs, states, *sent = found
    return fv, fs, cv, cs


def solution(mesh):
    field = P(None, "depth", "hx", "hy")
    ids = P("depth", "hx", "hy")
    return jax.shard_map(
        per_device,
        mesh=mesh,
        in_specs=(field,) * 4 + (P(None, None, "depth", "hx", "hy"),) + (ids,) * 3 + (P(),) * 5,
        out_specs=(field,) * 4,
        check_vma=False,
    )
```

```python
import functools

import jax
import jax.numpy as jnp
from jax import lax
from jax.experimental import pallas as pl
from jax.experimental.pallas import tpu as pltpu
from jax.sharding import PartitionSpec as P

DT = 0.4
NEAR = 9.0 / 8.0
FAR = 1.0 / 24.0
F32 = jnp.float32
NX, NZ, OWN, TILE = 6, 4, 384, 128
WIDE = OWN + TILE
CWIDE = 2 * TILE
STRESS = {"x": (0, 3, 4), "y": (1, 3, 5), "z": (2, 4, 5)}
SPEED = {"x": (0, 1, 2), "y": (0, 1, 2), "z": (0, 1, 2)}
FINE_TILES = (
    [(18, [("s", c) for c in range(3)]), (18, [("s", c) for c in range(3, 6)])]
    + [(12, [("v", 0), ("v", 1), ("v", 2), ("zone", None), ("plastic", None)])]
    + [(6, [("q", (n // 6, n % 6)) for n in range(10 * t, 10 * t + 10)]) for t in range(6)]
)
COARSE_TILES = [
    (8, [("s", c) for c in range(6)]),
    (8, [("v", 0), ("v", 1), ("v", 2), ("zone", None)]),
]
N_FINE = len(FINE_TILES)
Y_MESSAGE = (N_FINE * NX + len(COARSE_TILES), 4, TILE)
X_MESSAGE = (8, 4, WIDE)
Z_MESSAGE = (11, 4, WIDE)


def roll(x, shift, axis):
    shift %= x.shape[axis]
    return x if shift == 0 else pltpu.roll(x, shift, axis)


def iota(shape, axis):
    return lax.broadcasted_iota(jnp.int32, shape, axis)


def stencil(get, forward, scale):
    near, far = NEAR * scale, FAR * scale
    if forward:
        return near * (get(1) - get(0)) - far * (get(2) - get(-1))
    return near * (get(0) - get(-1)) - far * (get(1) - get(-2))


def lookup(zones, table):
    total = jnp.zeros(zones.shape, F32)
    for member in range(table.shape[0]):
        total = jnp.where(zones == float(member + 1), table[member], total)
    return total


def pack_y(get, width, names, rows, way):
    lane = iota((rows, TILE), 1)
    tile = jnp.zeros((rows, TILE), F32)
    for slot, name in enumerate(names):
        start = 2 * width * slot + (width if way == 0 else 0)
        edge = roll(get(name), 2 * width * slot + width, 1)
        tile = jnp.where((lane >= start) & (lane < start + width), edge, tile)
    return tile


def merged(before, after, width):
    lane = iota(before.shape, 1)
    return jnp.where(lane % (2 * width) < width, before, after)


def halo_of(tile, width, slot):
    return roll(tile, -(2 * width * slot + width), 1)


def pack_kernel(fs, fv, zone, plastic, states, cs, cv, czone, back, on):
    for way, out in ((0, back), (1, on)):
        lanes = slice(0, TILE) if way == 0 else slice(OWN - TILE, OWN)

        def fine(name, x):
            kind, c = name
            if kind == "s":
                return fs[c, x, :, lanes]
            if kind == "v":
                return fv[c, x, :, lanes]
            if kind == "q":
                return states[c[0], c[1], x, :, lanes]
            if kind == "zone":
                return zone[x, :, lanes].astype(F32) + 1.0
            return plastic[x, :, lanes].astype(F32)

        def pair(name, x):
            return jnp.concatenate([fine(name, x), fine(name, x + 1)], 0)

        for t, (width, names) in enumerate(FINE_TILES):
            for x in range(0, NX, 2):
                tile = pack_y(functools.partial(pair, x=x), width, names, 8, way)
                out[t * NX + x] = tile[0:4]
                out[t * NX + x + 1] = tile[4:8]

        def coarse(name):
            kind, c = name
            if kind == "zone":
                rows = [czone[1 - z].astype(F32) + 1.0 for z in range(2)]
            else:
                rows = [(cs if kind == "s" else cv)[c, 1 - z] for z in range(2)]
            return jnp.concatenate(rows * 2, 0)

        for t, (width, names) in enumerate(COARSE_TILES):
            out[N_FINE * NX + t] = pack_y(coarse, width, names, 8, way)[0:4]


def start_kernel(fs, fv, zone, plastic, cs, cv, czone, before, after, *rest):
    nfs, nfv, nzone, nplastic, ncs, ncv, nczone = rest[:7]
    for x in range(NX):
        for c in range(6):
            nfs[c, x, :, 0:OWN] = fs[c, x]
        for c in range(3):
            nfv[c, x, :, 0:OWN] = fv[c, x]
        nzone[x, :, 0:OWN] = zone[x].astype(F32) + 1.0
        nplastic[x, :, 0:OWN] = plastic[x].astype(F32)
    fine = {"s": nfs, "v": nfv, "zone": nzone, "plastic": nplastic}
    for t, (width, names) in enumerate(FINE_TILES[:3]):
        for x in range(0, NX, 2):
            at = t * NX + x
            two = [jnp.concatenate([m[at], m[at + 1]], 0) for m in (before, after)]
            tile = merged(two[0], two[1], width)
            for slot, (kind, c) in enumerate(names):
                halo = halo_of(tile, width, slot)
                for i in range(2):
                    to = (x + i,) if c is None else (c, x + i)
                    fine[kind][to + (slice(None), slice(OWN, WIDE))] = halo[4 * i : 4 * i + 4]
    for z in range(2):
        for c in range(6):
            ncs[c, z, :, 0:TILE] = cs[c, 1 - z]
        for c in range(3):
            ncv[c, z, :, 0:TILE] = cv[c, 1 - z]
        nczone[z, :, 0:TILE] = czone[1 - z].astype(F32) + 1.0
    coarse = {"s": ncs, "v": ncv, "zone": nczone}
    for t, (width, names) in enumerate(COARSE_TILES):
        two = [jnp.concatenate([m[N_FINE * NX + t]] * 2, 0) for m in (before, after)]
        tile = merged(two[0], two[1], width)
        for slot, (kind, c) in enumerate(names):
            halo = halo_of(tile, width, slot)
            for z in range(2):
                to = (z,) if c is None else (c, z)
                coarse[kind][to + (slice(None), slice(TILE, CWIDE))] = halo[2 * z : 2 * z + 2]
    pack(nfs, ncs, STRESS, rest[7:])


def pack(fine, coarse, sets, out):
    for way in range(2):
        to_x, to_z = out[way], out[2 + way]
        for place, c in enumerate(sets["x"]):
            for i in range(2):
                to_x[2 * place + i] = fine[c, 4 * way + i]
        for place, c in enumerate(sets["z"]):
            for x in range(NX):
                rows = slice(2 * (x % 2), 2 * (x % 2) + 2)
                to_z[3 * place + x // 2, rows] = fine[c, x, 2 * way : 2 * way + 2]
        for out_ref, first, comps in ((to_x, 6, sets["x"]), (to_z, 9, sets["z"])):
            for place, c in enumerate(comps):
                for z in range(2):
                    out_ref[first + place // 2, 2 * z : 2 * z + 2, coarse_lanes(place)] = coarse[c, z]
            out_ref[first + 1, :, CWIDE:WIDE] = jnp.zeros((4, CWIDE), F32)


def coarse_lanes(place):
    return slice(CWIDE * (place % 2), CWIDE * (place % 2) + CWIDE)


class Fields:
    def __init__(self, fine, coarse, sets, halos, rooms):
        self.fine, self.coarse, self.sets = fine, coarse, sets
        self.x_before, self.x_after, self.z_before, self.z_after = halos
        self.z_room, self.c_room, self.narrow_room, self.wide_room = rooms
        self.couple()
        for place, c in enumerate(sets["z"]):
            for x in range(NX):
                at, rows = 3 * place + x // 2, slice(2 * (x % 2), 2 * (x % 2) + 2)
                self.z_room[place, x, 0:4] = fine[c, x]
                self.z_room[place, x, 4:6] = self.z_after[at, rows] + self.below[c, x]
                self.z_room[place, x, 6:8] = self.z_before[at, rows]
        for c in range(coarse.shape[0]):
            for z in range(2):
                self.c_room[c, z, 0:2] = coarse[c, z]
                if c in sets["x"]:
                    place = sets["x"].index(c)
                    spot = (6 + place // 2, slice(2 * z, 2 * z + 2), coarse_lanes(place))
                    self.c_room[c, z, 2:4] = self.x_after[spot]
                    self.c_room[c, z, 6:8] = self.x_before[spot]
                else:
                    self.c_room[c, z, 2:8] = jnp.zeros((6, CWIDE), F32)

    def couple(self):
        bottom = (lax.axis_index("depth") == lax.axis_size("depth") - 1).astype(F32)
        comps = self.sets["z"]

        def match(shape, wide_axis):
            wide, narrow = iota(shape, wide_axis), iota(shape, 1 - wide_axis)
            first = jnp.where(narrow < CWIDE - TILE // 2, narrow, narrow - CWIDE) * 3
            wide = jnp.where(wide < WIDE - TILE // 2, wide, wide - WIDE)
            return (wide >= first) & (wide < first + 3)

        repeat = jnp.where(match((CWIDE, WIDE), 1), 1.0, 0.0).astype(F32)
        gather = jnp.where(match((WIDE, CWIDE), 0), bottom / 9.0, 0.0).astype(F32)
        dot = functools.partial(
            jnp.dot, precision=lax.Precision.HIGHEST, preferred_element_type=F32
        )
        narrow, wide = self.narrow_room, self.wide_room
        narrow[6:8] = jnp.zeros((2, CWIDE), F32)
        wide[12:16] = jnp.zeros((4, WIDE), F32)
        for place, c in enumerate(comps):
            narrow[2 * place : 2 * place + 2] = self.coarse[c, 0]
            for step, z in enumerate((3, 0)):
                for r in range(2):
                    at = 4 * place + 2 * step + r
                    line = [self.fine[c, 3 * r + i, z : z + 1] for i in range(3)]
                    wide[at : at + 1] = line[0] + line[1] + line[2]
        spread = dot(narrow[...], repeat)
        means = dot(wide[...], gather)
        self.below, self.above = {}, {}
        far = iota((2, WIDE), 0) == 1
        for place, c in enumerate(comps):
            for x in range(NX):
                last, line = self.fine[c, x, 3:4], spread[2 * place + x // 3 : 2 * place + x // 3 + 1]
                near, deep = 2.0 / 3.0 * last + 1.0 / 3.0 * line, 1.0 / 3.0 * last + 2.0 / 3.0 * line
                self.below[c, x] = bottom * jnp.where(far, deep, near)
            for step in range(2):
                at = 4 * place + 2 * step
                self.above[c, -1 - step] = means[at : at + 2]

    def fine_x(self, c, x):
        place = self.sets["x"].index(c)

        def get(off):
            at = x + off
            if at < 0:
                return self.x_before[2 * place + at + 2]
            if at >= NX:
                return self.x_after[2 * place + at - NX]
            return self.fine[c, at]

        return get

    def fine_y(self, c, x):
        first = x - x % 2
        both = jnp.concatenate([self.fine[c, first], self.fine[c, first + 1]], 0)
        rows = slice(4 * (x % 2), 4 * (x % 2) + 4)
        return lambda off: roll(both, -off, 1)[rows]

    def fine_z(self, c, x):
        whole = self.z_room[self.sets["z"].index(c), x]
        return lambda off: roll(whole, -off, 0)[0:4]

    def coarse_x(self, c, z):
        whole = self.c_room[c, z]
        return lambda off: roll(whole, -off, 0)[0:2]

    def coarse_y(self, c, z):
        whole = self.c_room[c, z]
        return lambda off: roll(whole, -off, 1)[0:2]

    def coarse_z(self, c, z):
        place = self.sets["z"].index(c)

        def piece(message, at):
            return message[9 + place // 2, 2 * at : 2 * at + 2, coarse_lanes(place)]

        def get(off):
            at = z + off
            if at < 0:
                return piece(self.z_after, at + 2) + self.above[c, at]
            if at < 2:
                return self.coarse[c, at]
            return piece(self.z_before, at - 2)

        return get

    def fine_ways(self, x):
        return [lambda c, of=of: of(c, x) for of in (self.fine_x, self.fine_y, self.fine_z)]

    def coarse_ways(self, z):
        return [lambda c, of=of: of(c, z) for of in (self.coarse_x, self.coarse_y, self.coarse_z)]


def forces(x, y, z, scale):
    def go(of, c, forward):
        return stencil(of(c), forward, scale)

    return (
        go(x, 0, True) + go(y, 3, False) + go(z, 4, False),
        go(x, 3, False) + go(y, 1, True) + go(z, 5, False),
        go(x, 4, False) + go(y, 5, False) + go(z, 2, True),
    )


def rates(x, y, z, scale):
    def go(of, c, forward):
        return stencil(of(c), forward, scale)

    return (
        go(x, 0, False),
        go(y, 1, False),
        go(z, 2, False),
        go(x, 1, True) + go(y, 0, True),
        go(x, 2, True) + go(z, 0, True),
        go(y, 2, True) + go(z, 1, True),
    )


def velocity_kernel(last, fv, cv, fs, cs, zone, czone, table, *rest):
    halos, rest = rest[:4], rest[4:]
    nfv, ncv, *out = rest[:6]
    f = Fields(fs, cs, STRESS, halos, rest[-4:])
    for x in range(NX):
        gain = DT * lookup(zone[x], table)
        found = forces(*f.fine_ways(x), 1.0)
        for c in range(3):
            new = fv[c, x] + gain * found[c]
            nfv[c, x] = new
            if last:
                rest[6][c, x] = new[:, 0:OWN]
    for z in range(2):
        gain = DT * lookup(czone[z], table)
        found = forces(*f.coarse_ways(z), 1.0 / 3.0)
        for c in range(3):
            new = cv[c, z] + gain * found[c]
            ncv[c, z] = new
            if last:
                rest[7][c, 1 - z] = new[:, 0:TILE]
    pack(nfv, ncv, SPEED, out)


def stress_kernel(last, fv, cv, fs, cs, zone, czone, plastic, states, *rest):
    before, after = (None, None) if last else rest[:2]
    rest = rest if last else rest[2:]
    lame, shear, share, radius = rest[:4]
    halos, rest = rest[4:8], rest[8:]
    nfs, ncs = rest[:2]
    f = Fields(fv, cv, SPEED, halos, rest[-4:])
    width = OWN if last else WIDE
    total = share[0]
    for k in range(1, share.shape[0]):
        total = total + share[k]
    per_share = 1.0 / jnp.full((4, TILE), total, F32)
    per_share = jnp.concatenate([per_share] * (width // TILE), 1)
    tiles = {}

    def state(k, c, x):
        own = states[k, c, x]
        if last:
            return own
        tile, slot = divmod(6 * k + c, 10)
        at = (3 + tile) * NX + x
        if (tile, x) not in tiles:
            first = at - x % 2
            two = [jnp.concatenate([m[first], m[first + 1]], 0) for m in (before, after)]
            tiles[tile, x] = merged(two[0], two[1], 6)
        halo = halo_of(tiles[tile, x], 6, slot)
        return jnp.concatenate([own, halo[4 * (x % 2) : 4 * (x % 2) + 4]], 1)

    for x in range(NX):
        e = [part[:, 0:width] for part in rates(*f.fine_ways(x), 1.0)]
        ids = zone[x, :, 0:width]
        first, mu = lookup(ids, lame), lookup(ids, shear)
        twice = (2.0 * DT) * mu
        once = DT * mu
        dilation = e[0] + e[1] + e[2]
        third = dilation * (1.0 / 3.0)
        old = [fs[c, x, :, 0:width] for c in range(6)]
        pressure = DT * first * dilation
        rise = [twice * e[c] for c in range(3)] + [once * e[c] for c in range(3, 6)]
        elastic = [old[c] + pressure + rise[c] for c in range(3)] + [old[c] + rise[c] for c in range(3, 6)]
        step = [twice * (e[c] - third) for c in range(3)] + rise[3:]
        step = [per_share * part for part in step]
        active = plastic[x, :, 0:width] == 1.0
        sums = [jnp.zeros((4, width), F32)] * 6
        for k in range(share.shape[0]):
            weight, limit = share[k], radius[k]
            was = [state(k, c, x) for c in range(6)]
            t = [was[c] + weight * step[c] for c in range(6)]
            size = 0.5 * (t[0] * t[0] + t[1] * t[1] + t[2] * t[2]) + (
                t[3] * t[3] + t[4] * t[4] + t[5] * t[5]
            )
            scale = limit * lax.rsqrt(jnp.maximum(size, limit * limit))
            t = [part * scale for part in t]
            sums = [a + b for a, b in zip(sums, t)]
            if not last:
                for c in range(6):
                    rest[2][k, c, x] = jnp.where(active, t[c], was[c])[:, 0:OWN]
        mean = (old[0] + old[1] + old[2]) * (1.0 / 3.0) + (DT * first + twice * (1.0 / 3.0)) * dilation
        for c in range(6):
            nfs[c, x] = jnp.where(active, mean + sums[c] if c < 3 else sums[c], elastic[c])
    for z in range(2):
        e = rates(*f.coarse_ways(z), 1.0 / 3.0)
        first, mu = lookup(czone[z], lame), lookup(czone[z], shear)
        pressure = DT * first * (e[0] + e[1] + e[2])
        for c in range(6):
            rise = (2.0 * DT if c < 3 else DT) * mu * e[c]
            new = cs[c, z] + (pressure + rise if c < 3 else rise)
            if last:
                ncs[c, 1 - z] = new[:, 0:TILE]
            else:
                ncs[c, z] = new
    if not last:
        pack(nfs, ncs, STRESS, rest[3:7])


VMEM = pl.BlockSpec(memory_space=pltpu.VMEM)
SMEM = pl.BlockSpec(memory_space=pltpu.SMEM)
SENT = [X_MESSAGE, X_MESSAGE, Z_MESSAGE, Z_MESSAGE]


def call(body, operands, scalars, halos, outs, fields, flops):
    rooms = [(3, NX, 8, WIDE), (fields, 2, 8, CWIDE), (8, CWIDE), (16, WIDE)] if fields else []
    return pl.pallas_call(
        body,
        out_shape=[jax.ShapeDtypeStruct(s, F32) for s in outs],
        in_specs=[VMEM] * len(operands) + [SMEM] * len(scalars) + [VMEM] * len(halos),
        out_specs=[VMEM] * len(outs),
        scratch_shapes=[pltpu.VMEM(s, F32) for s in rooms],
        compiler_params=pltpu.CompilerParams(vmem_limit_bytes=40 * 2**20),
        cost_estimate=pl.CostEstimate(flops=flops, bytes_accessed=flops, transcendentals=0),
    )(*operands, *scalars, *halos)


def exchange(axes, sent):
    found = []
    for number, axis in enumerate(axes):
        back, on = sent[2 * number : 2 * number + 2]
        up = [(i, i + 1) for i in range(lax.axis_size(axis) - 1)]
        found.append(lax.ppermute(on, axis, up))
        found.append(lax.ppermute(back, axis, [(b, a) for a, b in up]))
    return found


def per_device(fv, fs, cv, cs, states, zone, czone, plastic, buoyancy, lame, shear, share, radius):
    fv, fs, states, zone, plastic = [jnp.swapaxes(a, -3, -2) for a in (fv, fs, states, zone, plastic)]
    sent = call(pack_kernel, [fs, fv, zone, plastic, states, cs, cv, czone], [], [], [Y_MESSAGE] * 2, 0, 10**6)
    y_halo = exchange(["hy"], sent)
    grown = [(6, NX, 4, WIDE), (3, NX, 4, WIDE), (NX, 4, WIDE), (NX, 4, WIDE)]
    grown += [(6, 2, 2, CWIDE), (3, 2, 2, CWIDE), (2, 2, CWIDE)]
    fs, fv, zone, plastic, cs, cv, czone, *sent = call(
        start_kernel, [fs, fv, zone, plastic, cs, cv, czone], [], y_halo, grown + SENT, 0, 10**6
    )
    for step in range(2):
        last = step == 1
        outs = [fv.shape, cv.shape] + SENT + ([(3, NX, 4, OWN), (3, 2, 2, TILE)] if last else [])
        found = call(
            functools.partial(velocity_kernel, last),
            [fv, cv, fs, cs, zone, czone],
            [buoyancy],
            exchange(["hx", "depth"], sent),
            outs,
            6,
            10**6,
        )
        fv, cv, *sent = found[:6]
        if last:
            fv_out, cv_out = found[6:]
            outs = [(6, NX, 4, OWN), (6, 2, 2, TILE)]
        else:
            outs = [fs.shape, cs.shape, states.shape] + SENT
        found = call(
            functools.partial(stress_kernel, last),
            [fv, cv, fs, cs, zone, czone, plastic, states] + ([] if last else y_halo),
            [lame, shear, share, radius],
            exchange(["hx", "depth"], sent),
            outs,
            3,
            10**7,
        )
        if last:
            fs, cs = found
        else:
            fs, cs, states, *sent = found
    return jnp.swapaxes(fv_out, 1, 2), jnp.swapaxes(fs, 1, 2), cv_out, cs


def solution(mesh):
    field = P(None, "depth", "hx", "hy")
    ids = P("depth", "hx", "hy")
    return jax.shard_map(
        per_device,
        mesh=mesh,
        in_specs=(field,) * 4 + (P(None, None, "depth", "hx", "hy"),) + (ids,) * 3 + (P(),) * 5,
        out_specs=(field,) * 4,
        check_vma=False,
    )
```

```python
import functools

import jax
import jax.numpy as jnp
from jax import lax
from jax.experimental import pallas as pl
from jax.experimental.pallas import tpu as pltpu
from jax.sharding import PartitionSpec as P

DT = 0.4
NEAR = 9.0 / 8.0
FAR = 1.0 / 24.0
F32 = jnp.float32
NX, NZ, OWN, TILE = 6, 4, 384, 128
WIDE = OWN + TILE
CWIDE = 2 * TILE
STRESS = {"x": (0, 3, 4), "y": (1, 3, 5), "z": (2, 4, 5)}
SPEED = {"x": (0, 1, 2), "y": (0, 1, 2), "z": (0, 1, 2)}
FINE_TILES = (
    [(18, [("s", c) for c in range(3)]), (18, [("s", c) for c in range(3, 6)])]
    + [(12, [("v", 0), ("v", 1), ("v", 2), ("zone", None), ("plastic", None)])]
    + [(6, [("q", (n // 6, n % 6)) for n in range(10 * t, 10 * t + 10)]) for t in range(6)]
)
COARSE_TILES = [
    (8, [("s", c) for c in range(6)]),
    (8, [("v", 0), ("v", 1), ("v", 2), ("zone", None)]),
]
N_FINE = len(FINE_TILES)
Y_MESSAGE = (N_FINE * NX + len(COARSE_TILES), 4, TILE)
X_MESSAGE = (8, 4, WIDE)
Z_MESSAGE = (11, 4, WIDE)


def roll(x, shift, axis):
    shift %= x.shape[axis]
    return x if shift == 0 else pltpu.roll(x, shift, axis)


def iota(shape, axis):
    return lax.broadcasted_iota(jnp.int32, shape, axis)


def stencil(get, forward, scale):
    near, far = NEAR * scale, FAR * scale
    if forward:
        return near * (get(1) - get(0)) - far * (get(2) - get(-1))
    return near * (get(0) - get(-1)) - far * (get(1) - get(-2))


def lookup(zones, table):
    total = jnp.zeros(zones.shape, F32)
    for member in range(table.shape[0]):
        total = jnp.where(zones == float(member + 1), table[member], total)
    return total


def pack_y(get, width, names, rows, way):
    lane = iota((rows, TILE), 1)
    tile = jnp.zeros((rows, TILE), F32)
    for slot, name in enumerate(names):
        start = 2 * width * slot + (width if way == 0 else 0)
        edge = roll(get(name), 2 * width * slot + width, 1)
        tile = jnp.where((lane >= start) & (lane < start + width), edge, tile)
    return tile


def merged(before, after, width):
    lane = iota(before.shape, 1)
    return jnp.where(lane % (2 * width) < width, before, after)


def halo_of(tile, width, slot):
    return roll(tile, -(2 * width * slot + width), 1)


def pack_kernel(*refs):
    given, (back, on), held, arrived = refs[:8], refs[8:10], refs[10:18], refs[18]
    copies = [pltpu.make_async_copy(a, b, arrived.at[i]) for i, (a, b) in enumerate(zip(given, held))]
    for copy in copies:
        copy.start()
    for copy in copies:
        copy.wait()
    states, fs, fv, zone, plastic, cs, cv, czone = held
    for way, out in ((0, back), (1, on)):
        lanes = slice(0, TILE) if way == 0 else slice(OWN - TILE, OWN)

        def fine(name, x):
            kind, c = name
            if kind == "s":
                return fs[c, x, :, lanes]
            if kind == "v":
                return fv[c, x, :, lanes]
            if kind == "q":
                return states[c[0], c[1], x, :, lanes]
            if kind == "zone":
                return zone[x, :, lanes].astype(F32) + 1.0
            return plastic[x, :, lanes].astype(F32)

        def pair(name, x):
            return jnp.concatenate([fine(name, x), fine(name, x + 1)], 0)

        for t, (width, names) in enumerate(FINE_TILES):
            for x in range(0, NX, 2):
                tile = pack_y(functools.partial(pair, x=x), width, names, 8, way)
                out[t * NX + x] = tile[0:4]
                out[t * NX + x + 1] = tile[4:8]

        def coarse(name):
            kind, c = name
            if kind == "zone":
                rows = [czone[1 - z].astype(F32) + 1.0 for z in range(2)]
            else:
                rows = [(cs if kind == "s" else cv)[c, 1 - z] for z in range(2)]
            return jnp.concatenate(rows * 2, 0)

        for t, (width, names) in enumerate(COARSE_TILES):
            out[N_FINE * NX + t] = pack_y(coarse, width, names, 8, way)[0:4]


def start_kernel(fs, fv, zone, plastic, cs, cv, czone, before, after, *rest):
    nfs, nfv, nzone, nplastic, ncs, ncv, nczone = rest[:7]
    for x in range(NX):
        for c in range(6):
            nfs[c, x, :, 0:OWN] = fs[c, x]
        for c in range(3):
            nfv[c, x, :, 0:OWN] = fv[c, x]
        nzone[x, :, 0:OWN] = zone[x].astype(F32) + 1.0
        nplastic[x, :, 0:OWN] = plastic[x].astype(F32)
    fine = {"s": nfs, "v": nfv, "zone": nzone, "plastic": nplastic}
    for t, (width, names) in enumerate(FINE_TILES[:3]):
        for x in range(0, NX, 2):
            at = t * NX + x
            two = [jnp.concatenate([m[at], m[at + 1]], 0) for m in (before, after)]
            tile = merged(two[0], two[1], width)
            for slot, (kind, c) in enumerate(names):
                halo = halo_of(tile, width, slot)
                for i in range(2):
                    to = (x + i,) if c is None else (c, x + i)
                    fine[kind][to + (slice(None), slice(OWN, WIDE))] = halo[4 * i : 4 * i + 4]
    for z in range(2):
        for c in range(6):
            ncs[c, z, :, 0:TILE] = cs[c, 1 - z]
        for c in range(3):
            ncv[c, z, :, 0:TILE] = cv[c, 1 - z]
        nczone[z, :, 0:TILE] = czone[1 - z].astype(F32) + 1.0
    coarse = {"s": ncs, "v": ncv, "zone": nczone}
    for t, (width, names) in enumerate(COARSE_TILES):
        two = [jnp.concatenate([m[N_FINE * NX + t]] * 2, 0) for m in (before, after)]
        tile = merged(two[0], two[1], width)
        for slot, (kind, c) in enumerate(names):
            halo = halo_of(tile, width, slot)
            for z in range(2):
                to = (z,) if c is None else (c, z)
                coarse[kind][to + (slice(None), slice(TILE, CWIDE))] = halo[2 * z : 2 * z + 2]
    pack(nfs, ncs, STRESS, rest[7:])


def pack(fine, coarse, sets, out):
    for way in range(2):
        to_x, to_z = out[way], out[2 + way]
        for place, c in enumerate(sets["x"]):
            for i in range(2):
                to_x[2 * place + i] = fine[c, 4 * way + i]
        for place, c in enumerate(sets["z"]):
            for x in range(NX):
                rows = slice(2 * (x % 2), 2 * (x % 2) + 2)
                to_z[3 * place + x // 2, rows] = fine[c, x, 2 * way : 2 * way + 2]
        for out_ref, first, comps in ((to_x, 6, sets["x"]), (to_z, 9, sets["z"])):
            for place, c in enumerate(comps):
                for z in range(2):
                    out_ref[first + place // 2, 2 * z : 2 * z + 2, coarse_lanes(place)] = coarse[c, z]
            out_ref[first + 1, :, CWIDE:WIDE] = jnp.zeros((4, CWIDE), F32)


def coarse_lanes(place):
    return slice(CWIDE * (place % 2), CWIDE * (place % 2) + CWIDE)


class Fields:
    def __init__(self, fine, coarse, sets, halos, rooms):
        self.fine, self.coarse, self.sets = fine, coarse, sets
        self.x_before, self.x_after, self.z_before, self.z_after = halos
        self.z_room, self.c_room, self.narrow_room, self.wide_room = rooms
        self.couple()
        for place, c in enumerate(sets["z"]):
            for x in range(NX):
                at, rows = 3 * place + x // 2, slice(2 * (x % 2), 2 * (x % 2) + 2)
                self.z_room[place, x, 0:4] = fine[c, x]
                self.z_room[place, x, 4:6] = self.z_after[at, rows] + self.below[c, x]
                self.z_room[place, x, 6:8] = self.z_before[at, rows]
        for c in range(coarse.shape[0]):
            for z in range(2):
                self.c_room[c, z, 0:2] = coarse[c, z]
                if c in sets["x"]:
                    place = sets["x"].index(c)
                    spot = (6 + place // 2, slice(2 * z, 2 * z + 2), coarse_lanes(place))
                    self.c_room[c, z, 2:4] = self.x_after[spot]
                    self.c_room[c, z, 6:8] = self.x_before[spot]
                else:
                    self.c_room[c, z, 2:8] = jnp.zeros((6, CWIDE), F32)

    def couple(self):
        bottom = (lax.axis_index("depth") == lax.axis_size("depth") - 1).astype(F32)
        comps = self.sets["z"]

        def match(shape, wide_axis):
            wide, narrow = iota(shape, wide_axis), iota(shape, 1 - wide_axis)
            first = jnp.where(narrow < CWIDE - TILE // 2, narrow, narrow - CWIDE) * 3
            wide = jnp.where(wide < WIDE - TILE // 2, wide, wide - WIDE)
            return (wide >= first) & (wide < first + 3)

        repeat = jnp.where(match((CWIDE, WIDE), 1), 1.0, 0.0).astype(F32)
        gather = jnp.where(match((WIDE, CWIDE), 0), bottom / 9.0, 0.0).astype(F32)
        dot = functools.partial(
            jnp.dot, precision=lax.Precision.HIGHEST, preferred_element_type=F32
        )
        narrow, wide = self.narrow_room, self.wide_room
        narrow[6:8] = jnp.zeros((2, CWIDE), F32)
        wide[12:16] = jnp.zeros((4, WIDE), F32)
        for place, c in enumerate(comps):
            narrow[2 * place : 2 * place + 2] = self.coarse[c, 0]
            for step, z in enumerate((3, 0)):
                for r in range(2):
                    at = 4 * place + 2 * step + r
                    line = [self.fine[c, 3 * r + i, z : z + 1] for i in range(3)]
                    wide[at : at + 1] = line[0] + line[1] + line[2]
        spread = dot(narrow[...], repeat)
        means = dot(wide[...], gather)
        self.below, self.above = {}, {}
        far = iota((2, WIDE), 0) == 1
        for place, c in enumerate(comps):
            for x in range(NX):
                last, line = self.fine[c, x, 3:4], spread[2 * place + x // 3 : 2 * place + x // 3 + 1]
                near, deep = 2.0 / 3.0 * last + 1.0 / 3.0 * line, 1.0 / 3.0 * last + 2.0 / 3.0 * line
                self.below[c, x] = bottom * jnp.where(far, deep, near)
            for step in range(2):
                at = 4 * place + 2 * step
                self.above[c, -1 - step] = means[at : at + 2]

    def fine_x(self, c, x):
        place = self.sets["x"].index(c)

        def get(off):
            at = x + off
            if at < 0:
                return self.x_before[2 * place + at + 2]
            if at >= NX:
                return self.x_after[2 * place + at - NX]
            return self.fine[c, at]

        return get

    def fine_y(self, c, x):
        first = x - x % 2
        both = jnp.concatenate([self.fine[c, first], self.fine[c, first + 1]], 0)
        rows = slice(4 * (x % 2), 4 * (x % 2) + 4)
        return lambda off: roll(both, -off, 1)[rows]

    def fine_z(self, c, x):
        whole = self.z_room[self.sets["z"].index(c), x]
        return lambda off: roll(whole, -off, 0)[0:4]

    def coarse_x(self, c, z):
        whole = self.c_room[c, z]
        return lambda off: roll(whole, -off, 0)[0:2]

    def coarse_y(self, c, z):
        whole = self.c_room[c, z]
        return lambda off: roll(whole, -off, 1)[0:2]

    def coarse_z(self, c, z):
        place = self.sets["z"].index(c)

        def piece(message, at):
            return message[9 + place // 2, 2 * at : 2 * at + 2, coarse_lanes(place)]

        def get(off):
            at = z + off
            if at < 0:
                return piece(self.z_after, at + 2) + self.above[c, at]
            if at < 2:
                return self.coarse[c, at]
            return piece(self.z_before, at - 2)

        return get

    def fine_ways(self, x):
        return [lambda c, of=of: of(c, x) for of in (self.fine_x, self.fine_y, self.fine_z)]

    def coarse_ways(self, z):
        return [lambda c, of=of: of(c, z) for of in (self.coarse_x, self.coarse_y, self.coarse_z)]


def forces(x, y, z, scale):
    def go(of, c, forward):
        return stencil(of(c), forward, scale)

    return (
        go(x, 0, True) + go(y, 3, False) + go(z, 4, False),
        go(x, 3, False) + go(y, 1, True) + go(z, 5, False),
        go(x, 4, False) + go(y, 5, False) + go(z, 2, True),
    )


def rates(x, y, z, scale):
    def go(of, c, forward):
        return stencil(of(c), forward, scale)

    return (
        go(x, 0, False),
        go(y, 1, False),
        go(z, 2, False),
        go(x, 1, True) + go(y, 0, True),
        go(x, 2, True) + go(z, 0, True),
        go(y, 2, True) + go(z, 1, True),
    )


def velocity_kernel(last, fv, cv, fs, cs, zone, czone, table, *rest):
    halos, rest = rest[:4], rest[4:]
    nfv, ncv, *out = rest[:6]
    f = Fields(fs, cs, STRESS, halos, rest[-4:])
    for x in range(NX):
        gain = DT * lookup(zone[x], table)
        found = forces(*f.fine_ways(x), 1.0)
        for c in range(3):
            new = fv[c, x] + gain * found[c]
            nfv[c, x] = new
            if last:
                rest[6][c, x] = new[:, 0:OWN]
    for z in range(2):
        gain = DT * lookup(czone[z], table)
        found = forces(*f.coarse_ways(z), 1.0 / 3.0)
        for c in range(3):
            new = cv[c, z] + gain * found[c]
            ncv[c, z] = new
            if last:
                rest[7][c, 1 - z] = new[:, 0:TILE]
    pack(nfv, ncv, SPEED, out)


def stress_kernel(last, fv, cv, fs, cs, zone, czone, plastic, states, *rest):
    before, after = (None, None) if last else rest[:2]
    rest = rest if last else rest[2:]
    lame, shear, share, radius = rest[:4]
    halos, rest = rest[4:8], rest[8:]
    nfs, ncs = rest[:2]
    f = Fields(fv, cv, SPEED, halos, rest[-4:])
    width = OWN if last else WIDE
    total = share[0]
    for k in range(1, share.shape[0]):
        total = total + share[k]
    per_share = 1.0 / jnp.full((4, TILE), total, F32)
    per_share = jnp.concatenate([per_share] * (width // TILE), 1)
    tiles = {}

    def state(k, c, x):
        own = states[k, c, x]
        if last:
            return own
        tile, slot = divmod(6 * k + c, 10)
        at = (3 + tile) * NX + x
        if (tile, x) not in tiles:
            first = at - x % 2
            two = [jnp.concatenate([m[first], m[first + 1]], 0) for m in (before, after)]
            tiles[tile, x] = merged(two[0], two[1], 6)
        halo = halo_of(tiles[tile, x], 6, slot)
        return jnp.concatenate([own, halo[4 * (x % 2) : 4 * (x % 2) + 4]], 1)

    for x in range(NX):
        e = [part[:, 0:width] for part in rates(*f.fine_ways(x), 1.0)]
        ids = zone[x, :, 0:width]
        first, mu = lookup(ids, lame), lookup(ids, shear)
        twice = (2.0 * DT) * mu
        once = DT * mu
        dilation = e[0] + e[1] + e[2]
        third = dilation * (1.0 / 3.0)
        old = [fs[c, x, :, 0:width] for c in range(6)]
        pressure = DT * first * dilation
        rise = [twice * e[c] for c in range(3)] + [once * e[c] for c in range(3, 6)]
        elastic = [old[c] + pressure + rise[c] for c in range(3)] + [old[c] + rise[c] for c in range(3, 6)]
        step = [twice * (e[c] - third) for c in range(3)] + rise[3:]
        step = [per_share * part for part in step]
        active = plastic[x, :, 0:width] == 1.0
        sums = [jnp.zeros((4, width), F32)] * 6
        for k in range(share.shape[0]):
            weight, limit = share[k], radius[k]
            was = [state(k, c, x) for c in range(6)]
            t = [was[c] + weight * step[c] for c in range(6)]
            size = 0.5 * (t[0] * t[0] + t[1] * t[1] + t[2] * t[2]) + (
                t[3] * t[3] + t[4] * t[4] + t[5] * t[5]
            )
            scale = limit * lax.rsqrt(jnp.maximum(size, limit * limit))
            t = [part * scale for part in t]
            sums = [a + b for a, b in zip(sums, t)]
            if not last:
                for c in range(6):
                    rest[2][k, c, x] = jnp.where(active, t[c], was[c])[:, 0:OWN]
        mean = (old[0] + old[1] + old[2]) * (1.0 / 3.0) + (DT * first + twice * (1.0 / 3.0)) * dilation
        for c in range(6):
            nfs[c, x] = jnp.where(active, mean + sums[c] if c < 3 else sums[c], elastic[c])
    for z in range(2):
        e = rates(*f.coarse_ways(z), 1.0 / 3.0)
        first, mu = lookup(czone[z], lame), lookup(czone[z], shear)
        pressure = DT * first * (e[0] + e[1] + e[2])
        for c in range(6):
            rise = (2.0 * DT if c < 3 else DT) * mu * e[c]
            new = cs[c, z] + (pressure + rise if c < 3 else rise)
            if last:
                ncs[c, 1 - z] = new[:, 0:TILE]
            else:
                ncs[c, z] = new
    if not last:
        pack(nfs, ncs, STRESS, rest[3:7])


VMEM = pl.BlockSpec(memory_space=pltpu.VMEM)
SMEM = pl.BlockSpec(memory_space=pltpu.SMEM)
SENT = [X_MESSAGE, X_MESSAGE, Z_MESSAGE, Z_MESSAGE]


def call(body, operands, scalars, halos, outs, fields, flops):
    rooms = [(3, NX, 8, WIDE), (fields, 2, 8, CWIDE), (8, CWIDE), (16, WIDE)] if fields else []
    return pl.pallas_call(
        body,
        out_shape=[jax.ShapeDtypeStruct(s, F32) for s in outs],
        in_specs=[VMEM] * len(operands) + [SMEM] * len(scalars) + [VMEM] * len(halos),
        out_specs=[VMEM] * len(outs),
        scratch_shapes=[pltpu.VMEM(s, F32) for s in rooms],
        compiler_params=pltpu.CompilerParams(vmem_limit_bytes=40 * 2**20),
        cost_estimate=pl.CostEstimate(flops=flops, bytes_accessed=flops, transcendentals=0),
    )(*operands, *scalars, *halos)


def exchange(axes, sent):
    found = []
    for number, axis in enumerate(axes):
        back, on = sent[2 * number : 2 * number + 2]
        up = [(i, i + 1) for i in range(lax.axis_size(axis) - 1)]
        found.append(lax.ppermute(on, axis, up))
        found.append(lax.ppermute(back, axis, [(b, a) for a, b in up]))
    return found


def per_device(fv, fs, cv, cs, states, zone, czone, plastic, buoyancy, lame, shear, share, radius):
    fv, fs, states, zone, plastic = [jnp.swapaxes(a, -3, -2) for a in (fv, fs, states, zone, plastic)]
    given = [states, fs, fv, zone, plastic, cs, cv, czone]
    sent = pl.pallas_call(
        pack_kernel,
        out_shape=[jax.ShapeDtypeStruct(Y_MESSAGE, F32)] * 2,
        in_specs=[pl.BlockSpec(memory_space=pltpu.HBM)] * len(given),
        out_specs=[VMEM] * 2,
        scratch_shapes=[pltpu.VMEM(a.shape, a.dtype) for a in given]
        + [pltpu.SemaphoreType.DMA((len(given),))],
        compiler_params=pltpu.CompilerParams(vmem_limit_bytes=60 * 2**20),
        cost_estimate=pl.CostEstimate(flops=10**6, bytes_accessed=10**6, transcendentals=0),
    )(*given)
    y_halo = exchange(["hy"], sent)
    grown = [(6, NX, 4, WIDE), (3, NX, 4, WIDE), (NX, 4, WIDE), (NX, 4, WIDE)]
    grown += [(6, 2, 2, CWIDE), (3, 2, 2, CWIDE), (2, 2, CWIDE)]
    fs, fv, zone, plastic, cs, cv, czone, *sent = call(
        start_kernel, [fs, fv, zone, plastic, cs, cv, czone], [], y_halo, grown + SENT, 0, 10**6
    )
    for step in range(2):
        last = step == 1
        outs = [fv.shape, cv.shape] + SENT + ([(3, NX, 4, OWN), (3, 2, 2, TILE)] if last else [])
        found = call(
            functools.partial(velocity_kernel, last),
            [fv, cv, fs, cs, zone, czone],
            [buoyancy],
            exchange(["hx", "depth"], sent),
            outs,
            6,
            10**6,
        )
        fv, cv, *sent = found[:6]
        if last:
            fv_out, cv_out = found[6:]
            outs = [(6, NX, 4, OWN), (6, 2, 2, TILE)]
        else:
            outs = [fs.shape, cs.shape, states.shape] + SENT
        found = call(
            functools.partial(stress_kernel, last),
            [fv, cv, fs, cs, zone, czone, plastic, states] + ([] if last else y_halo),
            [lame, shear, share, radius],
            exchange(["hx", "depth"], sent),
            outs,
            3,
            10**7,
        )
        if last:
            fs, cs = found
        else:
            fs, cs, states, *sent = found
    return jnp.swapaxes(fv_out, 1, 2), jnp.swapaxes(fs, 1, 2), cv_out, cs


def solution(mesh):
    field = P(None, "depth", "hx", "hy")
    ids = P("depth", "hx", "hy")
    return jax.shard_map(
        per_device,
        mesh=mesh,
        in_specs=(field,) * 4 + (P(None, None, "depth", "hx", "hy"),) + (ids,) * 3 + (P(),) * 5,
        out_specs=(field,) * 4,
        check_vma=False,
    )
```

```python
import functools

import jax
import jax.numpy as jnp
from jax import lax
from jax.experimental import pallas as pl
from jax.experimental.pallas import tpu as pltpu
from jax.sharding import PartitionSpec as P

DT = 0.4
NEAR = 9.0 / 8.0
FAR = 1.0 / 24.0
F32 = jnp.float32
NX, NZ, OWN, TILE = 6, 4, 384, 128
WIDE = OWN + TILE
CWIDE = 2 * TILE
STRESS = {"x": (0, 3, 4), "y": (1, 3, 5), "z": (2, 4, 5)}
SPEED = {"x": (0, 1, 2), "y": (0, 1, 2), "z": (0, 1, 2)}
FINE_TILES = (
    [(18, [("s", c) for c in range(3)]), (18, [("s", c) for c in range(3, 6)])]
    + [(12, [("v", 0), ("v", 1), ("v", 2), ("zone", None), ("plastic", None)])]
    + [(6, [("q", (n // 6, n % 6)) for n in range(10 * t, 10 * t + 10)]) for t in range(6)]
)
COARSE_TILES = [
    (8, [("s", c) for c in range(6)]),
    (8, [("v", 0), ("v", 1), ("v", 2), ("zone", None)]),
]
N_FINE = len(FINE_TILES)
Y_MESSAGE = (N_FINE * NX + len(COARSE_TILES), 4, TILE)
X_MESSAGE = (8, 4, WIDE)
Z_MESSAGE = (11, 4, WIDE)


def roll(x, shift, axis):
    shift %= x.shape[axis]
    return x if shift == 0 else pltpu.roll(x, shift, axis)


def iota(shape, axis):
    return lax.broadcasted_iota(jnp.int32, shape, axis)


def stencil(get, forward, scale):
    near, far = NEAR * scale, FAR * scale
    if forward:
        return near * (get(1) - get(0)) - far * (get(2) - get(-1))
    return near * (get(0) - get(-1)) - far * (get(1) - get(-2))


def lookup(zones, table):
    total = jnp.zeros(zones.shape, F32)
    for member in range(table.shape[0]):
        total = jnp.where(zones == float(member + 1), table[member], total)
    return total


def pack_y(get, width, names, rows, way):
    lane = iota((rows, TILE), 1)
    tile = jnp.zeros((rows, TILE), F32)
    for slot, name in enumerate(names):
        start = 2 * width * slot + (width if way == 0 else 0)
        edge = roll(get(name), 2 * width * slot + width, 1)
        tile = jnp.where((lane >= start) & (lane < start + width), edge, tile)
    return tile


def merged(before, after, width):
    lane = iota(before.shape, 1)
    return jnp.where(lane % (2 * width) < width, before, after)


def halo_of(tile, width, slot):
    return roll(tile, -(2 * width * slot + width), 1)


def between_grids(shape, wide_axis):
    wide, narrow = iota(shape, wide_axis), iota(shape, 1 - wide_axis)
    first = jnp.where(narrow < CWIDE - TILE // 2, narrow, narrow - CWIDE) * 3
    wide = jnp.where(wide < WIDE - TILE // 2, wide, wide - WIDE)
    return jnp.where((wide >= first) & (wide < first + 3), 1.0, 0.0).astype(jnp.bfloat16)


def in_pieces(x, ones):
    high = x.astype(jnp.bfloat16).astype(F32)
    rest = x - high
    middle = rest.astype(jnp.bfloat16).astype(F32)
    pieces = jnp.concatenate([high, middle, rest - middle], 0).astype(jnp.bfloat16)
    out = jnp.dot(pieces, ones, preferred_element_type=F32)
    return out[0:16] + out[16:32] + out[32:48]


def pack_kernel(*refs):
    given, (back, on, repeat, gather), held, arrived = refs[:8], refs[8:12], refs[12:20], refs[20]
    copies = [pltpu.make_async_copy(a, b, arrived.at[i]) for i, (a, b) in enumerate(zip(given, held))]
    for copy in copies:
        copy.start()
    repeat[...] = between_grids((CWIDE, WIDE), 1)
    gather[...] = between_grids((WIDE, CWIDE), 0)
    for copy in copies:
        copy.wait()
    states, fs, fv, zone, plastic, cs, cv, czone = held
    for way, out in ((0, back), (1, on)):
        lanes = slice(0, TILE) if way == 0 else slice(OWN - TILE, OWN)

        def fine(name, x):
            kind, c = name
            if kind == "s":
                return fs[c, x, :, lanes]
            if kind == "v":
                return fv[c, x, :, lanes]
            if kind == "q":
                return states[c[0], c[1], x, :, lanes]
            if kind == "zone":
                return zone[x, :, lanes].astype(F32) + 1.0
            return plastic[x, :, lanes].astype(F32)

        def pair(name, x):
            return jnp.concatenate([fine(name, x), fine(name, x + 1)], 0)

        for t, (width, names) in enumerate(FINE_TILES):
            for x in range(0, NX, 2):
                tile = pack_y(functools.partial(pair, x=x), width, names, 8, way)
                out[t * NX + x] = tile[0:4]
                out[t * NX + x + 1] = tile[4:8]

        def coarse(name):
            kind, c = name
            if kind == "zone":
                rows = [czone[1 - z].astype(F32) + 1.0 for z in range(2)]
            else:
                rows = [(cs if kind == "s" else cv)[c, 1 - z] for z in range(2)]
            return jnp.concatenate(rows * 2, 0)

        for t, (width, names) in enumerate(COARSE_TILES):
            out[N_FINE * NX + t] = pack_y(coarse, width, names, 8, way)[0:4]


def start_kernel(fs, fv, zone, plastic, cs, cv, czone, before, after, *rest):
    nfs, nfv, nzone, nplastic, ncs, ncv, nczone = rest[:7]
    for x in range(NX):
        for c in range(6):
            nfs[c, x, :, 0:OWN] = fs[c, x]
        for c in range(3):
            nfv[c, x, :, 0:OWN] = fv[c, x]
        nzone[x, :, 0:OWN] = zone[x].astype(F32) + 1.0
        nplastic[x, :, 0:OWN] = plastic[x].astype(F32)
    fine = {"s": nfs, "v": nfv, "zone": nzone, "plastic": nplastic}
    for t, (width, names) in enumerate(FINE_TILES[:3]):
        for x in range(0, NX, 2):
            at = t * NX + x
            two = [jnp.concatenate([m[at], m[at + 1]], 0) for m in (before, after)]
            tile = merged(two[0], two[1], width)
            for slot, (kind, c) in enumerate(names):
                halo = halo_of(tile, width, slot)
                for i in range(2):
                    to = (x + i,) if c is None else (c, x + i)
                    fine[kind][to + (slice(None), slice(OWN, WIDE))] = halo[4 * i : 4 * i + 4]
    for z in range(2):
        for c in range(6):
            ncs[c, z, :, 0:TILE] = cs[c, 1 - z]
        for c in range(3):
            ncv[c, z, :, 0:TILE] = cv[c, 1 - z]
        nczone[z, :, 0:TILE] = czone[1 - z].astype(F32) + 1.0
    coarse = {"s": ncs, "v": ncv, "zone": nczone}
    for t, (width, names) in enumerate(COARSE_TILES):
        two = [jnp.concatenate([m[N_FINE * NX + t]] * 2, 0) for m in (before, after)]
        tile = merged(two[0], two[1], width)
        for slot, (kind, c) in enumerate(names):
            halo = halo_of(tile, width, slot)
            for z in range(2):
                to = (z,) if c is None else (c, z)
                coarse[kind][to + (slice(None), slice(TILE, CWIDE))] = halo[2 * z : 2 * z + 2]
    pack(nfs, ncs, STRESS, rest[7:])


def pack(fine, coarse, sets, out):
    for way in range(2):
        to_x, to_z = out[way], out[2 + way]
        for place, c in enumerate(sets["x"]):
            for i in range(2):
                to_x[2 * place + i] = fine[c, 4 * way + i]
        for place, c in enumerate(sets["z"]):
            for x in range(NX):
                rows = slice(2 * (x % 2), 2 * (x % 2) + 2)
                to_z[3 * place + x // 2, rows] = fine[c, x, 2 * way : 2 * way + 2]
        for out_ref, first, comps in ((to_x, 6, sets["x"]), (to_z, 9, sets["z"])):
            for place, c in enumerate(comps):
                for z in range(2):
                    out_ref[first + place // 2, 2 * z : 2 * z + 2, coarse_lanes(place)] = coarse[c, z]
            out_ref[first + 1, :, CWIDE:WIDE] = jnp.zeros((4, CWIDE), F32)


def coarse_lanes(place):
    return slice(CWIDE * (place % 2), CWIDE * (place % 2) + CWIDE)


class Fields:
    def __init__(self, fine, coarse, sets, maps, halos, rooms):
        self.repeat, self.gather = maps
        self.fine, self.coarse, self.sets = fine, coarse, sets
        self.x_before, self.x_after, self.z_before, self.z_after = halos
        self.z_room, self.c_room, self.narrow_room, self.wide_room = rooms
        self.couple()
        for place, c in enumerate(sets["z"]):
            for x in range(NX):
                at, rows = 3 * place + x // 2, slice(2 * (x % 2), 2 * (x % 2) + 2)
                self.z_room[place, x, 0:4] = fine[c, x]
                self.z_room[place, x, 4:6] = self.z_after[at, rows] + self.below[c, x]
                self.z_room[place, x, 6:8] = self.z_before[at, rows]
        for c in range(coarse.shape[0]):
            for z in range(2):
                self.c_room[c, z, 0:2] = coarse[c, z]
                if c in sets["x"]:
                    place = sets["x"].index(c)
                    spot = (6 + place // 2, slice(2 * z, 2 * z + 2), coarse_lanes(place))
                    self.c_room[c, z, 2:4] = self.x_after[spot]
                    self.c_room[c, z, 6:8] = self.x_before[spot]
                else:
                    self.c_room[c, z, 2:8] = jnp.zeros((6, CWIDE), F32)

    def couple(self):
        bottom = (lax.axis_index("depth") == lax.axis_size("depth") - 1).astype(F32)
        comps = self.sets["z"]

        narrow, wide = self.narrow_room, self.wide_room
        narrow[6:16] = jnp.zeros((10, CWIDE), F32)
        wide[12:16] = jnp.zeros((4, WIDE), F32)
        for place, c in enumerate(comps):
            narrow[2 * place : 2 * place + 2] = self.coarse[c, 0]
            for step, z in enumerate((3, 0)):
                for r in range(2):
                    at = 4 * place + 2 * step + r
                    line = [self.fine[c, 3 * r + i, z : z + 1] for i in range(3)]
                    wide[at : at + 1] = line[0] + line[1] + line[2]
        spread = in_pieces(narrow[...], self.repeat[...])
        means = in_pieces(wide[...], self.gather[...]) * (bottom / 9.0)
        self.below, self.above = {}, {}
        far = iota((2, WIDE), 0) == 1
        for place, c in enumerate(comps):
            for x in range(NX):
                last, line = self.fine[c, x, 3:4], spread[2 * place + x // 3 : 2 * place + x // 3 + 1]
                near, deep = 2.0 / 3.0 * last + 1.0 / 3.0 * line, 1.0 / 3.0 * last + 2.0 / 3.0 * line
                self.below[c, x] = bottom * jnp.where(far, deep, near)
            for step in range(2):
                at = 4 * place + 2 * step
                self.above[c, -1 - step] = means[at : at + 2]

    def fine_x(self, c, x):
        place = self.sets["x"].index(c)

        def get(off):
            at = x + off
            if at < 0:
                return self.x_before[2 * place + at + 2]
            if at >= NX:
                return self.x_after[2 * place + at - NX]
            return self.fine[c, at]

        return get

    def fine_y(self, c, x):
        first = x - x % 2
        both = jnp.concatenate([self.fine[c, first], self.fine[c, first + 1]], 0)
        rows = slice(4 * (x % 2), 4 * (x % 2) + 4)
        return lambda off: roll(both, -off, 1)[rows]

    def fine_z(self, c, x):
        whole = self.z_room[self.sets["z"].index(c), x]
        return lambda off: roll(whole, -off, 0)[0:4]

    def coarse_x(self, c, z):
        whole = self.c_room[c, z]
        return lambda off: roll(whole, -off, 0)[0:2]

    def coarse_y(self, c, z):
        whole = self.c_room[c, z]
        return lambda off: roll(whole, -off, 1)[0:2]

    def coarse_z(self, c, z):
        place = self.sets["z"].index(c)

        def piece(message, at):
            return message[9 + place // 2, 2 * at : 2 * at + 2, coarse_lanes(place)]

        def get(off):
            at = z + off
            if at < 0:
                return piece(self.z_after, at + 2) + self.above[c, at]
            if at < 2:
                return self.coarse[c, at]
            return piece(self.z_before, at - 2)

        return get

    def fine_ways(self, x):
        return [lambda c, of=of: of(c, x) for of in (self.fine_x, self.fine_y, self.fine_z)]

    def coarse_ways(self, z):
        return [lambda c, of=of: of(c, z) for of in (self.coarse_x, self.coarse_y, self.coarse_z)]


def forces(x, y, z, scale):
    def go(of, c, forward):
        return stencil(of(c), forward, scale)

    return (
        go(x, 0, True) + go(y, 3, False) + go(z, 4, False),
        go(x, 3, False) + go(y, 1, True) + go(z, 5, False),
        go(x, 4, False) + go(y, 5, False) + go(z, 2, True),
    )


def rates(x, y, z, scale):
    def go(of, c, forward):
        return stencil(of(c), forward, scale)

    return (
        go(x, 0, False),
        go(y, 1, False),
        go(z, 2, False),
        go(x, 1, True) + go(y, 0, True),
        go(x, 2, True) + go(z, 0, True),
        go(y, 2, True) + go(z, 1, True),
    )


def velocity_kernel(fv, cv, fs, cs, zone, czone, repeat, gather, table, *rest):
    halos, rest = rest[:4], rest[4:]
    nfv, ncv, *out = rest[:6]
    f = Fields(fs, cs, STRESS, (repeat, gather), halos, rest[-4:])
    for x in range(NX):
        gain = DT * lookup(zone[x], table)
        found = forces(*f.fine_ways(x), 1.0)
        for c in range(3):
            nfv[c, x] = fv[c, x] + gain * found[c]
    for z in range(2):
        gain = DT * lookup(czone[z], table)
        found = forces(*f.coarse_ways(z), 1.0 / 3.0)
        for c in range(3):
            ncv[c, z] = cv[c, z] + gain * found[c]
    pack(nfv, ncv, SPEED, out)


def stress_kernel(last, fv, cv, fs, cs, zone, czone, repeat, gather, plastic, states, *rest):
    before, after = (None, None) if last else rest[:2]
    rest = rest if last else rest[2:]
    lame, shear, share, radius = rest[:4]
    halos, rest = rest[4:8], rest[8:]
    nfs, ncs = rest[:2]
    f = Fields(fv, cv, SPEED, (repeat, gather), halos, rest[4 if last else 7 :][:4])
    if last:
        sending = pltpu.make_async_copy(fv.at[:, :, :, 0:OWN], rest[2], rest[8].at[0])
        sending.start()
        for c in range(3):
            for z in range(2):
                rest[3][c, 1 - z] = cv[c, z, :, 0:TILE]
    width = OWN if last else WIDE
    total = share[0]
    for k in range(1, share.shape[0]):
        total = total + share[k]
    per_share = 1.0 / jnp.full((4, TILE), total, F32)
    per_share = jnp.concatenate([per_share] * (width // TILE), 1)
    tiles = {}

    def state(k, c, x):
        own = states[k, c, x]
        if last:
            return own
        tile, slot = divmod(6 * k + c, 10)
        at = (3 + tile) * NX + x
        if (tile, x) not in tiles:
            first = at - x % 2
            two = [jnp.concatenate([m[first], m[first + 1]], 0) for m in (before, after)]
            tiles[tile, x] = merged(two[0], two[1], 6)
        halo = halo_of(tiles[tile, x], 6, slot)
        return jnp.concatenate([own, halo[4 * (x % 2) : 4 * (x % 2) + 4]], 1)

    for x in range(NX):
        e = [part[:, 0:width] for part in rates(*f.fine_ways(x), 1.0)]
        ids = zone[x, :, 0:width]
        first, mu = lookup(ids, lame), lookup(ids, shear)
        twice = (2.0 * DT) * mu
        once = DT * mu
        dilation = e[0] + e[1] + e[2]
        third = dilation * (1.0 / 3.0)
        old = [fs[c, x, :, 0:width] for c in range(6)]
        pressure = DT * first * dilation
        rise = [twice * e[c] for c in range(3)] + [once * e[c] for c in range(3, 6)]
        elastic = [old[c] + pressure + rise[c] for c in range(3)] + [old[c] + rise[c] for c in range(3, 6)]
        step = [twice * (e[c] - third) for c in range(3)] + rise[3:]
        step = [per_share * part for part in step]
        active = plastic[x, :, 0:width] == 1.0
        sums = [jnp.zeros((4, width), F32)] * 6
        for k in range(share.shape[0]):
            weight, limit = share[k], radius[k]
            was = [state(k, c, x) for c in range(6)]
            t = [was[c] + weight * step[c] for c in range(6)]
            size = 0.5 * (t[0] * t[0] + t[1] * t[1] + t[2] * t[2]) + (
                t[3] * t[3] + t[4] * t[4] + t[5] * t[5]
            )
            scale = limit * lax.rsqrt(jnp.maximum(size, limit * limit))
            t = [part * scale for part in t]
            sums = [a + b for a, b in zip(sums, t)]
            if not last:
                for c in range(6):
                    rest[2][k, c, x] = jnp.where(active, t[c], was[c])[:, 0:OWN]
        mean = (old[0] + old[1] + old[2]) * (1.0 / 3.0) + (DT * first + twice * (1.0 / 3.0)) * dilation
        for c in range(6):
            nfs[c, x] = jnp.where(active, mean + sums[c] if c < 3 else sums[c], elastic[c])
    for z in range(2):
        e = rates(*f.coarse_ways(z), 1.0 / 3.0)
        first, mu = lookup(czone[z], lame), lookup(czone[z], shear)
        pressure = DT * first * (e[0] + e[1] + e[2])
        for c in range(6):
            rise = (2.0 * DT if c < 3 else DT) * mu * e[c]
            new = cs[c, z] + (pressure + rise if c < 3 else rise)
            if last:
                ncs[c, 1 - z] = new[:, 0:TILE]
            else:
                ncs[c, z] = new
    if last:
        sending.wait()
    else:
        pack(nfs, ncs, STRESS, rest[3:7])


VMEM = pl.BlockSpec(memory_space=pltpu.VMEM)
SMEM = pl.BlockSpec(memory_space=pltpu.SMEM)
SENT = [X_MESSAGE, X_MESSAGE, Z_MESSAGE, Z_MESSAGE]


def call(body, operands, scalars, halos, outs, fields, flops, direct=()):
    rooms = [(3, NX, 8, WIDE), (fields, 2, 8, CWIDE), (16, CWIDE), (16, WIDE)] if fields else []
    return pl.pallas_call(
        body,
        out_shape=[jax.ShapeDtypeStruct(s, F32) for s in outs],
        in_specs=[VMEM] * len(operands) + [SMEM] * len(scalars) + [VMEM] * len(halos),
        out_specs=[pl.BlockSpec(memory_space=pltpu.HBM) if i in direct else VMEM for i in range(len(outs))],
        scratch_shapes=[pltpu.VMEM(s, F32) for s in rooms]
        + ([pltpu.SemaphoreType.DMA((len(direct),))] if direct else []),
        compiler_params=pltpu.CompilerParams(vmem_limit_bytes=40 * 2**20),
        cost_estimate=pl.CostEstimate(flops=flops, bytes_accessed=flops, transcendentals=0),
    )(*operands, *scalars, *halos)


def exchange(axes, sent):
    found = []
    for number, axis in enumerate(axes):
        back, on = sent[2 * number : 2 * number + 2]
        up = [(i, i + 1) for i in range(lax.axis_size(axis) - 1)]
        found.append(lax.ppermute(on, axis, up))
        found.append(lax.ppermute(back, axis, [(b, a) for a, b in up]))
    return found


def per_device(fv, fs, cv, cs, states, zone, czone, plastic, buoyancy, lame, shear, share, radius):
    fv, fs, states, zone, plastic = [jnp.swapaxes(a, -3, -2) for a in (fv, fs, states, zone, plastic)]
    given = [states, fs, fv, zone, plastic, cs, cv, czone]
    *sent, repeat, gather = pl.pallas_call(
        pack_kernel,
        out_shape=[jax.ShapeDtypeStruct(Y_MESSAGE, F32)] * 2
        + [jax.ShapeDtypeStruct(s, jnp.bfloat16) for s in ((CWIDE, WIDE), (WIDE, CWIDE))],
        in_specs=[pl.BlockSpec(memory_space=pltpu.HBM)] * len(given),
        out_specs=[VMEM] * 4,
        scratch_shapes=[pltpu.VMEM(a.shape, a.dtype) for a in given]
        + [pltpu.SemaphoreType.DMA((len(given),))],
        compiler_params=pltpu.CompilerParams(vmem_limit_bytes=60 * 2**20),
        cost_estimate=pl.CostEstimate(flops=10**6, bytes_accessed=10**6, transcendentals=0),
    )(*given)
    y_halo = exchange(["hy"], sent)
    grown = [(6, NX, 4, WIDE), (3, NX, 4, WIDE), (NX, 4, WIDE), (NX, 4, WIDE)]
    grown += [(6, 2, 2, CWIDE), (3, 2, 2, CWIDE), (2, 2, CWIDE)]
    fs, fv, zone, plastic, cs, cv, czone, *sent = call(
        start_kernel, [fs, fv, zone, plastic, cs, cv, czone], [], y_halo, grown + SENT, 0, 10**6
    )
    for step in range(2):
        last = step == 1
        fv, cv, *sent = call(
            velocity_kernel,
            [fv, cv, fs, cs, zone, czone, repeat, gather],
            [buoyancy],
            exchange(["hx", "depth"], sent),
            [fv.shape, cv.shape] + SENT,
            6,
            10**6,
        )
        if last:
            outs = [(6, NX, 4, OWN), (6, 2, 2, TILE), (3, NX, 4, OWN), (3, 2, 2, TILE)]
        else:
            outs = [fs.shape, cs.shape, states.shape] + SENT
        found = call(
            functools.partial(stress_kernel, last),
            [fv, cv, fs, cs, zone, czone, repeat, gather, plastic, states] + ([] if last else y_halo),
            [lame, shear, share, radius],
            exchange(["hx", "depth"], sent),
            outs,
            3,
            10**7,
            (2,) if last else (),
        )
        if last:
            fs, cs, fv, cv = found
        else:
            fs, cs, states, *sent = found
    return jnp.swapaxes(fv, 1, 2), jnp.swapaxes(fs, 1, 2), cv, cs


def solution(mesh):
    field = P(None, "depth", "hx", "hy")
    ids = P("depth", "hx", "hy")
    return jax.shard_map(
        per_device,
        mesh=mesh,
        in_specs=(field,) * 4 + (P(None, None, "depth", "hx", "hy"),) + (ids,) * 3 + (P(),) * 5,
        out_specs=(field,) * 4,
        check_vma=False,
    )
```
